512 devices in a mesh: kv: 8 (over y), seq: 64 (over z, x, core).
Axes of the slice: x: 4, y: 8, z: 8, core: 2. Of those that a mesh axis runs over, the one named last changes fastest.
Arguments:
- queries: bfloat16 [128, 8192], P('seq', 'kv'), may hold values from -8 to 8
- owner_slot: int32 [128], replicated, may hold values from 0 to 127, each once
- suffix_len: int32 [128], P('seq'), may hold values from 1 to 256, as said below
- prompt_keys: bfloat16 [32768, 1024], P('seq', 'kv'), may hold values from -8 to 8
- prompt_value_rows: bfloat16 [32768, 1024], P('seq', 'kv'), may hold values from -6 to 6
- key_scale: float32 [256, 8], P('seq', 'kv'), may hold values from 0.5 to 3
- value_block_scale: float32 [256, 8], P('seq', 'kv'), may hold values from 0.5 to 2
- suffix_key_rows: bfloat16 [128, 256, 1024], P('seq', None, 'kv'), may hold values from -16 to 16
- suffix_value_rows: bfloat16 [128, 256, 1024], P('seq', None, 'kv'), may hold values from -6 to 6
- out_weight: bfloat16 [8192, 5120], P('kv', 'seq'), may hold values from -0.0625 to 0.0625
Outputs:
- layer_out: float32 [128, 5120], P('kv', 'seq')
The draws below stay inside these ranges and needn't reach their ends.
Inputs may be any that keep to these rules, and one draw needn't show every extreme that they name: `owner_slot`: each slot appears once; slot i belongs to index i // 2 of seq. Slot i's suffix occupies positions 0 to suffix_len[i] - 1; some slot has all 256.
All inputs are finite; a program needn't handle non-finite values.
Results may differ from the reference program's by a relative error of at most 0.0055.
Values may be sent and summed in bfloat16 or wider, within the bound.
A program may use at most 192 MiB of HBM per device.

```python
import math
import jax
import jax.numpy as jnp
from jax import lax

D = 5120
HEAD_WIDTH = 128
GROUP = 8
SUFFIX_LIMIT = 256
SCALE_SPAN = 128
KEY_HEADS = 8
HQ = 64
SAMPLE_COUNT = 128
PROMPT_LENGTH = 32768
SCALE_BLOCKS = 256


def draw_queries(key, part):
    key = jax.random.fold_in(key, 1)
    sampled_draws = jax.random.truncated_normal(key, -6.0, 6.0, (SAMPLE_COUNT, HQ * HEAD_WIDTH), jnp.float32)
    return sampled_draws.astype(jnp.bfloat16)


def draw_prompt_keys(key, part):
    key = jax.random.fold_in(key, 2)
    sampled_draws = jax.random.truncated_normal(key, -6.0, 6.0, (PROMPT_LENGTH, KEY_HEADS * HEAD_WIDTH), jnp.float32)
    return sampled_draws.astype(jnp.bfloat16)


def draw_key_scale(key, part):
    key = jax.random.fold_in(key, 3)
    sampled_draws = jnp.exp(jax.random.uniform(key, (PROMPT_LENGTH // SCALE_SPAN, KEY_HEADS), jnp.float32, math.log(0.5), math.log(3.0)))
    return sampled_draws


def draw_suffix_len(key, part):
    key = jax.random.fold_in(key, 4)
    lengths = jax.random.randint(key, (SAMPLE_COUNT,), 1, SUFFIX_LIMIT + 1, dtype=jnp.int32)
    full_slot = jax.random.randint(jax.random.fold_in(key, 5), (), 0, SAMPLE_COUNT, dtype=jnp.int32)
    return lengths.at[full_slot].set(SUFFIX_LIMIT)


def steps_of(own_key, extent, shards, least, high):
    level = 1.0
    for dim, parts in shards:
        steps = jax.random.uniform(jax.random.fold_in(jax.random.fold_in(own_key, 6), dim), (parts,), jnp.float32, least / len(shards), high / len(shards))
        level = level * jnp.repeat(jnp.exp(steps), extent[dim] // parts).reshape((-1,) + (1,) * (len(extent) - 1 - dim))
    return level


def bell_draw(rng, dims, width, reach, shards=(), kind=jnp.bfloat16):
    loudness = steps_of(rng, dims, shards, -0.22, 0.18) if shards else 1.0
    entries = jax.random.normal(rng, dims, jnp.float32) * width * loudness
    return jnp.minimum(jnp.maximum(entries, -reach), reach).astype(kind)


def setup_inputs(seed: int = 0) -> dict:
    key_list = jax.random.split(jax.random.key(seed), 11)
    queries = draw_queries(jax.random.fold_in(key_list[10], 71), 0)
    owner_slot = jax.random.permutation(key_list[1], SAMPLE_COUNT).astype(jnp.int32)
    suffix_len = draw_suffix_len(jax.random.fold_in(key_list[10], 71), 0)
    prompt_keys = draw_prompt_keys(jax.random.fold_in(key_list[10], 71), 0)
    prompt_value_rows = bell_draw(key_list[4], (PROMPT_LENGTH, KEY_HEADS * HEAD_WIDTH), 1.0, 6.0, ((0, 64), (1, 8)))
    key_scale = draw_key_scale(jax.random.fold_in(key_list[10], 71), 0)
    value_block_scale = jnp.clip(jnp.exp(math.log(2.0) - 1.3862944 * jax.random.uniform(key_list[6], (SCALE_BLOCKS, KEY_HEADS), jnp.float32) ** steps_of(key_list[6], (SCALE_BLOCKS, KEY_HEADS), ((0, 64), (1, 8)), -0.2, 0.2)), 0.5, 2.0)
    suffix_key_rows = bell_draw(key_list[7], (SAMPLE_COUNT, SUFFIX_LIMIT, KEY_HEADS * HEAD_WIDTH), 4.0, 16.0, ((0, 64), (2, 8)))
    suffix_value_rows = bell_draw(key_list[8], (SAMPLE_COUNT, SUFFIX_LIMIT, KEY_HEADS * HEAD_WIDTH), 1.0, 6.0, ((0, 64), (2, 8)))
    out_weight = bell_draw(key_list[9], (HQ * HEAD_WIDTH, D), (HQ * HEAD_WIDTH) ** -0.5, 0.0625, ((0, 8), (1, 64)))
    return dict(queries=queries, owner_slot=owner_slot, suffix_len=suffix_len, prompt_keys=prompt_keys, prompt_value_rows=prompt_value_rows, key_scale=key_scale, value_block_scale=value_block_scale, suffix_key_rows=suffix_key_rows, suffix_value_rows=suffix_value_rows, out_weight=out_weight)


NEG_FILL = -1.0e30


def reference(queries, owner_slot, suffix_len, prompt_keys, prompt_value_rows, key_scale, value_block_scale, suffix_key_rows, suffix_value_rows, out_weight):
    slot_sample = jnp.zeros((SAMPLE_COUNT,), jnp.int32).at[owner_slot].set(jnp.arange(SAMPLE_COUNT, dtype=jnp.int32))
    slot_queries = queries[slot_sample]
    inv_root = HEAD_WIDTH ** -0.5
    sample_span = min(SAMPLE_COUNT, max(1, 512 // GROUP))
    live_index = jnp.arange(SUFFIX_LIMIT, dtype=jnp.int32)

    def single_head(kv_head):
        col_start = (kv_head * HEAD_WIDTH).astype(jnp.int32)
        key_rows = lax.dynamic_slice_in_dim(prompt_keys, col_start, HEAD_WIDTH, 1).astype(jnp.float32)
        value_rows = lax.dynamic_slice_in_dim(prompt_value_rows, col_start, HEAD_WIDTH, 1).astype(jnp.float32)
        key_factor = lax.dynamic_slice_in_dim(key_scale, kv_head, 1, 1)[:, 0] * inv_root
        value_factor = lax.dynamic_slice_in_dim(value_block_scale, kv_head, 1, 1)[:, 0]
        group_queries = lax.dynamic_slice_in_dim(slot_queries, (kv_head * GROUP * HEAD_WIDTH).astype(jnp.int32), GROUP * HEAD_WIDTH, 1)

        def one_block(block_index):
            own_first = (block_index * sample_span).astype(jnp.int32)
            block_queries = lax.dynamic_slice_in_dim(group_queries, own_first, sample_span, 0).astype(jnp.float32)
            row_count = sample_span * GROUP
            scores = jnp.dot(block_queries.reshape(row_count, HEAD_WIDTH), key_rows.T)
            scores = (scores.reshape(row_count, SCALE_BLOCKS, SCALE_SPAN) * key_factor[None, :, None]).reshape(row_count, PROMPT_LENGTH)
            near_keys = lax.dynamic_slice_in_dim(lax.dynamic_slice_in_dim(suffix_key_rows, own_first, sample_span, 0), col_start, HEAD_WIDTH, 2).astype(jnp.float32)
            near_values = lax.dynamic_slice_in_dim(lax.dynamic_slice_in_dim(suffix_value_rows, own_first, sample_span, 0), col_start, HEAD_WIDTH, 2).astype(jnp.float32)
            lengths = lax.dynamic_slice_in_dim(suffix_len, own_first, sample_span, 0)
            near_scores = jnp.einsum("sjd,sud->sju", block_queries.reshape(sample_span, GROUP, HEAD_WIDTH), near_keys) * inv_root
            live_mask = live_index[None, None, :] < lengths[:, None, None]
            near_scores = jnp.where(live_mask, near_scores, NEG_FILL)
            peak = jnp.maximum(jnp.max(scores, axis=1).reshape(sample_span, GROUP), jnp.max(near_scores, axis=2))
            weights = jnp.exp(scores - peak.reshape(row_count)[:, None])
            near_weights = jnp.where(live_mask, jnp.exp(near_scores - peak[..., None]), 0.0)
            weight_sum = jnp.sum(weights, axis=1).reshape(sample_span, GROUP) + jnp.sum(near_weights, axis=2)
            scaled = (weights.reshape(row_count, SCALE_BLOCKS, SCALE_SPAN) * value_factor[None, :, None]).reshape(row_count, PROMPT_LENGTH).astype(jnp.bfloat16)
            scaled = lax.optimization_barrier(scaled).astype(jnp.float32)
            near_scaled = lax.optimization_barrier(near_weights.astype(jnp.bfloat16)).astype(jnp.float32)
            numerator = jnp.dot(scaled, value_rows).reshape(sample_span, GROUP, HEAD_WIDTH)
            numerator = numerator + jnp.einsum("sju,sud->sjd", near_scaled, near_values)
            return (numerator / weight_sum[..., None]).astype(jnp.bfloat16).reshape(sample_span, GROUP * HEAD_WIDTH)

        blocks_out = lax.map(one_block, jnp.arange(SAMPLE_COUNT // sample_span, dtype=jnp.int32))
        return blocks_out.reshape(SAMPLE_COUNT, GROUP * HEAD_WIDTH)

    each_head_part = lax.map(single_head, jnp.arange(KEY_HEADS, dtype=jnp.int32))
    attention = jnp.transpose(each_head_part, (1, 0, 2)).reshape(SAMPLE_COUNT, HQ * HEAD_WIDTH)
    return jnp.dot(attention, out_weight, preferred_element_type=jnp.float32)
```

```python
import functools

import jax
import jax.numpy as jnp
from jax import lax
from jax.experimental import pallas as pl
from jax.experimental.pallas import tpu as pltpu
from jax.sharding import PartitionSpec as P

MESH = pl.DeviceIdType.MESH
F32 = jnp.float32
BF16 = jnp.bfloat16
LOG2E = 1.4426950408889634
NEG_FILL = -1e30

CORES = 2
GROUP = 8
WIDTH = 128
OWN = 2
ROWS = OWN * GROUP
SPAN = 128

SQ, SC, SK, SV, SW, SF, SN, SS, SA, SY = range(10)
LQ, LO, LK, LV, LKS, LVS, LW, LSK, LSV, LSL = range(10)


def nt_dot(a, b):
    return lax.dot_general(a, b, (((1,), (1,)), ((), ())), preferred_element_type=F32)


def kernel(
    chips,
    groups,
    q_hbm,
    os_hbm,
    sl_hbm,
    k_hbm,
    v_hbm,
    ks_hbm,
    vs_hbm,
    sk_hbm,
    sv_hbm,
    w_hbm,
    o_ref,
    qown,
    osv,
    sls,
    kbuf,
    vbuf,
    ksv,
    vsv,
    scb,
    skb,
    svb,
    wbuf,
    q32,
    qg,
    qf32,
    qs32,
    nsend,
    ssend,
    nrecv,
    srecv,
    att,
    a32,
    ysend,
    yrecv,
    ssem,
    rsem,
    lsem,
):
    me = lax.axis_index("seq")
    y = lax.axis_index("kv")
    c = lax.rem(me, CORES)
    chip = me // CORES
    other = 1 - c

    def load(src, dst, i):
        cp = pltpu.make_async_copy(src, dst, lsem.at[i])
        cp.start()
        return cp

    def remote(src, dst, i, seq, kv):
        return pltpu.make_async_remote_copy(
            src_ref=src,
            dst_ref=dst,
            send_sem=ssem.at[i],
            recv_sem=rsem.at[i],
            device_id={"kv": kv, "seq": seq},
            device_id_type=MESH,
        )

    load_q = load(q_hbm, qown, LQ)
    load_o = load(os_hbm, osv, LO)
    load_ks = load(ks_hbm, ksv, LKS)
    load_vs = load(vs_hbm, vsv, LVS)
    load_k = load(k_hbm, kbuf.at[c], LK)
    load_v = load(v_hbm, vbuf.at[c], LV)
    load_w = load(w_hbm, wbuf.at[c], LW)
    load_sk = load(sk_hbm, skb, LSK)
    load_sv = load(sv_hbm, svb, LSV)
    load_sl = load(sl_hbm, sls, LSL)

    barrier = pltpu.get_barrier_semaphore()

    def greet(seq, kv):
        pl.semaphore_signal(barrier, inc=1, device_id={"kv": kv, "seq": seq}, device_id_type=MESH)

    def greet_plane(k, carry):
        greet(lax.rem(chip + k, chips) * CORES + c, y)
        return carry

    lax.fori_loop(1, chips, greet_plane, 0)

    def greet_column(k, carry):
        greet(chip * CORES + c, lax.rem(y + k, groups))
        greet(chip * CORES + other, lax.rem(y + k, groups))
        return carry

    lax.fori_loop(1, groups, greet_column, 0)
    greet(chip * CORES + other, y)

    load_q.wait()
    for h in range(GROUP):
        piece = qown[:, h * WIDTH : (h + 1) * WIDTH].astype(F32)
        for s in range(OWN):
            q32[s * GROUP + h : s * GROUP + h + 1, :] = piece[s : s + 1, :]
    qg[c, chip] = q32[...].astype(BF16)

    pl.semaphore_wait(barrier, (chips - 1) + 2 * (groups - 1) + 1)

    half = chips // 2

    def far_first(k):
        step = half - (k // 2)
        return lax.rem(jnp.where(lax.rem(k, 2) == 0, step, chips - step), chips)

    def send_queries(k, carry):
        t = lax.rem(chip + far_first(k), chips)
        remote(qg.at[c, chip], qg.at[c, chip], SQ, t * CORES + c, y).start()
        return carry

    lax.fori_loop(1, chips, send_queries, 0)

    partner = chip * CORES + other
    swap_k = remote(k_hbm, kbuf.at[c], SK, partner, y)
    swap_k.start()
    swap_v = remote(v_hbm, vbuf.at[c], SV, partner, y)
    swap_v.start()
    swap_w = remote(w_hbm, wbuf.at[c], SW, partner, y)
    swap_w.start()
    load_ks.wait()
    load_vs.wait()
    blocks = ksv.shape[0]
    scb[c, 0:blocks, :] = jnp.broadcast_to(ksv[...] * (WIDTH**-0.5 * LOG2E), (blocks, WIDTH))
    scb[c, blocks : 2 * blocks, :] = jnp.broadcast_to(vsv[...], (blocks, WIDTH))
    swap_f = remote(scb.at[c], scb.at[c], SF, partner, y)
    swap_f.start()

    load_o.wait()
    samples = chips * CORES * OWN
    slots = chips * OWN
    s_i = lax.broadcasted_iota(jnp.int32, (samples, samples), 0)
    m_i = lax.broadcasted_iota(jnp.int32, (samples, samples), 1)
    m_in = lax.rem(m_i, slots)
    s_of_m = (m_in // OWN) * (CORES * OWN) + (m_i // slots) * OWN + lax.rem(m_i, OWN)
    spread = jnp.where(s_i == s_of_m, 1.0, 0.0).astype(BF16)
    owner_rows = jnp.broadcast_to(osv[...].astype(F32), (16, samples)).astype(BF16)
    owner = jnp.dot(owner_rows, spread, preferred_element_type=F32)[0:1, :]
    i_i = lax.broadcasted_iota(jnp.int32, (slots, samples), 0)
    slot_i = (i_i // OWN) * (CORES * OWN) + c * OWN + lax.rem(i_i, OWN)
    pick = jnp.where(owner == slot_i.astype(F32), 1.0, 0.0).astype(BF16)

    many_q = qg.at[0, pl.ds(0, chips - 1)]
    remote(many_q, many_q, SQ, partner, y).wait_recv()
    swap_q = remote(qg.at[c], qg.at[c], SC, partner, y)
    swap_q.start()
    swap_q.wait_recv()

    qf32[...] = qg[...].reshape(samples * GROUP, WIDTH).astype(F32)
    by_head = jnp.concatenate(
        [qf32[pl.ds(h, samples, stride=GROUP), :].astype(BF16) for h in range(GROUP)], axis=1
    )
    picked = jnp.dot(pick, by_head, preferred_element_type=F32)
    for h in range(GROUP):
        qs32[pl.ds(h, slots, stride=GROUP), :] = picked[:, h * WIDTH : (h + 1) * WIDTH]

    load_k.wait()
    load_v.wait()
    swap_k.wait_recv()
    swap_v.wait_recv()
    swap_f.wait_recv()

    chunk_chips = 8
    chunk = chunk_chips * ROWS
    chunks = chips // chunk_chips
    row_in = lax.rem(lax.broadcasted_iota(jnp.int32, (chunk, WIDTH), 0), ROWS)
    lane = lax.broadcasted_iota(jnp.int32, (chunk, WIDTH), 1)

    def prompt_chunk(n):
        first = pl.multiple_of(n * chunk, chunk)
        qc = qs32[pl.ds(first, chunk), :].astype(BF16)
        parts = []
        for core in range(CORES):
            s = nt_dot(qc, kbuf[core])
            for b in range(blocks):
                parts.append(s[:, b * SPAN : (b + 1) * SPAN] * scb[core, b : b + 1, :])
        peak = functools.reduce(jnp.maximum, parts)
        peak = jnp.max(peak, axis=1, keepdims=True)
        parts = [jnp.exp2(s - peak) for s in parts]
        total = jnp.sum(functools.reduce(jnp.add, parts), axis=1, keepdims=True)
        numer = None
        for core in range(CORES):
            scaled = jnp.concatenate(
                [
                    (parts[core * blocks + b] * scb[core, blocks + b : blocks + b + 1, :]).astype(BF16)
                    for b in range(blocks)
                ],
                axis=1,
            )
            term = jnp.dot(scaled, vbuf[core], preferred_element_type=F32)
            numer = term if numer is None else numer + term
        nsend[pl.ds(first, chunk), :] = numer.astype(BF16)
        stats = jnp.where(lane == row_in, peak, 0.0) + jnp.where(lane == row_in + ROWS, total, 0.0)
        stats = jnp.sum(stats.reshape(chunk_chips, ROWS, WIDTH), axis=1)
        for i in range(chunk_chips):
            ssend[n * chunk_chips + i] = stats[i : i + 1, :]

    def send_partial(t):
        first = pl.multiple_of(t * ROWS, ROWS)
        remote(ssend.at[t], srecv.at[chip], SS, t * CORES + c, y).start()
        remote(nsend.at[pl.ds(first, ROWS)], nrecv.at[chip], SN, t * CORES + c, y).start()

    own_chunk = chip // chunk_chips

    def chunk_step(k, carry):
        off = lax.rem(k + chunks // 2, chunks)
        n = lax.rem(own_chunk + off, chunks)
        prompt_chunk(n)

        def send_one(i, inner):
            t = n * chunk_chips + i

            @pl.when(t != chip)
            def _():
                send_partial(t)

            return inner

        lax.fori_loop(0, chunk_chips, send_one, 0)
        return carry

    lax.fori_loop(0, chunks, chunk_step, 0)
    own_first = pl.multiple_of(chip * ROWS, ROWS)
    nrecv[chip] = nsend[pl.ds(own_first, ROWS), :]
    srecv[chip] = ssend[chip]

    load_sk.wait()
    load_sv.wait()
    load_sl.wait()
    own_q = qs32[pl.ds(own_first, ROWS), :].astype(BF16)
    limit = skb.shape[1]
    live_i = lax.broadcasted_iota(jnp.int32, (GROUP, limit), 1)
    near_numer, near_peak, near_total = [], [], []
    for j in range(OWN):
        live = live_i < sls[j]
        s = nt_dot(own_q, skb[j])[j * GROUP : (j + 1) * GROUP, :] * (WIDTH**-0.5 * LOG2E)
        s = jnp.where(live, s, NEG_FILL)
        peak = jnp.max(s, axis=1, keepdims=True)
        w = jnp.where(live, jnp.exp2(s - peak), 0.0)
        near_total.append(jnp.sum(w, axis=1, keepdims=True))
        near_peak.append(peak)
        w16 = jnp.concatenate([w, jnp.zeros_like(w)], axis=0).astype(BF16)
        near_numer.append(jnp.dot(w16, svb[j], preferred_element_type=F32)[:GROUP])
    near_numer = jnp.concatenate(near_numer, axis=0)
    near_peak = jnp.concatenate(near_peak, axis=0)
    near_total = jnp.concatenate(near_total, axis=0)

    many_s = srecv.at[pl.ds(0, chips - 1)]
    remote(many_s, many_s, SS, partner, y).wait_recv()
    stats = jnp.concatenate([srecv[i] for i in range(chips)], axis=0)
    stats = jnp.concatenate([stats, jnp.zeros((WIDTH - chips, WIDTH), F32)], axis=0)
    stats = jnp.transpose(stats)
    peaks = stats[0:ROWS, 0:chips]
    totals = stats[ROWS : 2 * ROWS, 0:chips]
    peak = jnp.maximum(jnp.max(peaks, axis=1, keepdims=True), near_peak)
    factor = jnp.exp2(peaks - peak)
    near_factor = jnp.exp2(near_peak - peak)
    total = jnp.sum(factor * totals, axis=1, keepdims=True) + near_total * near_factor
    many_n = nrecv.at[pl.ds(0, chips - 1)]
    remote(many_n, many_n, SN, partner, y).wait_recv()
    numer = near_numer * near_factor
    for i in range(chips):
        numer = numer + nrecv[i].astype(F32) * factor[:, i : i + 1]
    att[chip] = (numer / total).astype(BF16)

    def send_att(k, carry):
        t = lax.rem(chip + far_first(k), chips)
        remote(att.at[chip], att.at[chip], SA, t * CORES + c, y).start()
        return carry

    lax.fori_loop(1, chips, send_att, 0)
    load_w.wait()
    swap_w.wait_recv()
    many_a = att.at[pl.ds(0, chips - 1)]
    remote(many_a, many_a, SA, partner, y).wait_recv()

    a32[...] = att[...].reshape(slots * GROUP, WIDTH).astype(F32)
    rows = jnp.concatenate(
        [a32[pl.ds(h, slots, stride=GROUP), :].astype(BF16) for h in range(GROUP)], axis=1
    )
    per_group = slots // groups
    for core in range(CORES):
        part = jnp.dot(rows, wbuf[core], preferred_element_type=F32)
        ysend[core] = part.reshape(groups, per_group, part.shape[1])

    def send_out(k, carry):
        t = lax.rem(y + k, groups)
        remote(ysend.at[c, t], yrecv.at[c * groups + y], SY, chip * CORES + c, t).start()
        remote(ysend.at[other, t], yrecv.at[c * groups + y], SY, chip * CORES + other, t).start()
        return carry

    lax.fori_loop(1, groups, send_out, 0)
    remote(ysend.at[other, y], yrecv.at[c * groups + y], SY, partner, y).start()
    yrecv[c * groups + y] = ysend[c, y]
    many_y = yrecv.at[pl.ds(0, CORES * groups - 1)]
    last = remote(many_y, many_y, SY, partner, y)
    last.wait_recv()
    for core in range(CORES):
        acc = yrecv[core * groups]
        for i in range(1, groups):
            acc = acc + yrecv[core * groups + i]
        for q in range(per_group // OWN):
            first = q * CORES * OWN + core * OWN
            o_ref[first : first + OWN, :] = acc[q * OWN : (q + 1) * OWN, :]

    remote(many_q, many_q, SQ, partner, y).wait_send()
    swap_q.wait_send()
    swap_k.wait_send()
    swap_v.wait_send()
    swap_w.wait_send()
    swap_f.wait_send()
    remote(many_s, many_s, SS, partner, y).wait_send()
    remote(many_n, many_n, SN, partner, y).wait_send()
    remote(many_a, many_a, SA, partner, y).wait_send()
    last.wait_send()


def local(
    queries,
    owner_slot,
    suffix_len,
    prompt_keys,
    prompt_value_rows,
    key_scale,
    value_block_scale,
    suffix_key_rows,
    suffix_value_rows,
    out_weight,
):
    groups = lax.axis_size("kv")
    chips = lax.axis_size("seq") // CORES
    samples = chips * CORES * OWN
    slots = chips * OWN
    positions = prompt_keys.shape[0]
    blocks = key_scale.shape[0]
    limit = suffix_key_rows.shape[1]
    depth, columns = out_weight.shape
    out_rows = samples // groups
    any_spec = pl.BlockSpec(memory_space=pl.ANY)
    return pl.pallas_call(
        functools.partial(kernel, chips, groups),
        out_shape=jax.ShapeDtypeStruct((out_rows, columns), F32),
        in_specs=[any_spec] * 10,
        out_specs=pl.BlockSpec(memory_space=pltpu.VMEM),
        scratch_shapes=[
            pltpu.VMEM(queries.shape, BF16),
            pltpu.VMEM((1, samples), jnp.int32),
            pltpu.SMEM((OWN,), jnp.int32),
            pltpu.VMEM((CORES, positions, WIDTH), BF16),
            pltpu.VMEM((CORES, positions, WIDTH), BF16),
            pltpu.VMEM((blocks, 1), F32),
            pltpu.VMEM((blocks, 1), F32),
            pltpu.VMEM((CORES, 2 * blocks, WIDTH), F32),
            pltpu.VMEM((OWN, limit, WIDTH), BF16),
            pltpu.VMEM((OWN, limit, WIDTH), BF16),
            pltpu.VMEM((CORES, depth, columns), BF16),
            pltpu.VMEM((ROWS, WIDTH), F32),
            pltpu.VMEM((CORES, chips, ROWS, WIDTH), BF16),
            pltpu.VMEM((samples * GROUP, WIDTH), F32),
            pltpu.VMEM((slots * GROUP, WIDTH), F32),
            pltpu.VMEM((slots * GROUP, WIDTH), BF16),
            pltpu.VMEM((chips, 1, WIDTH), F32),
            pltpu.VMEM((chips, ROWS, WIDTH), BF16),
            pltpu.VMEM((chips, 1, WIDTH), F32),
            pltpu.VMEM((chips, ROWS, WIDTH), BF16),
            pltpu.VMEM((slots * GROUP, WIDTH), F32),
            pltpu.VMEM((CORES, groups, slots // groups, columns), F32),
            pltpu.VMEM((CORES * groups, slots // groups, columns), F32),
            pltpu.SemaphoreType.DMA((10,)),
            pltpu.SemaphoreType.DMA((10,)),
            pltpu.SemaphoreType.DMA((10,)),
        ],
        compiler_params=pltpu.CompilerParams(
            collective_id=0, has_side_effects=True, vmem_limit_bytes=32 * 1024 * 1024
        ),
        name="decode_attention",
    )(
        queries,
        owner_slot.reshape(1, samples),
        suffix_len,
        prompt_keys,
        prompt_value_rows,
        key_scale,
        value_block_scale,
        suffix_key_rows,
        suffix_value_rows,
        out_weight,
    )


def solution(mesh):
    in_specs = (
        P("seq", "kv"),
        P(),
        P("seq"),
        P("seq", "kv"),
        P("seq", "kv"),
        P("seq", "kv"),
        P("seq", "kv"),
        P("seq", None, "kv"),
        P("seq", None, "kv"),
        P("kv", "seq"),
    )
    out_specs = P("kv", "seq")
    return jax.shard_map(local, mesh=mesh, in_specs=in_specs, out_specs=out_specs, check_vma=False)
```

```python
import functools

import jax
import jax.numpy as jnp
from jax import lax
from jax.experimental import pallas as pl
from jax.experimental.pallas import tpu as pltpu
from jax.sharding import PartitionSpec as P

MESH = pl.DeviceIdType.MESH
F32 = jnp.float32
BF16 = jnp.bfloat16
LOG2E = 1.4426950408889634
NEG_FILL = -1e30

CORES = 2
ROW_CHIPS = 4
GROUP = 8
WIDTH = 128
OWN = 2
ROWS = OWN * GROUP
SPAN = 128

SQ, SC, SK, SV, SW, SF, SN, SS, SA, SY = range(10)
LQ, LO, LK, LV, LKS, LVS, LW, LSK, LSV, LSL = range(10)


def nt_dot(a, b):
    return lax.dot_general(a, b, (((1,), (1,)), ((), ())), preferred_element_type=F32)


def kernel(
    chips,
    groups,
    q_hbm,
    os_hbm,
    sl_hbm,
    k_hbm,
    v_hbm,
    ks_hbm,
    vs_hbm,
    sk_hbm,
    sv_hbm,
    w_hbm,
    o_ref,
    qown,
    osv,
    sls,
    kbuf,
    vbuf,
    ksv,
    vsv,
    scb,
    skb,
    svb,
    wbuf,
    q32,
    qg,
    qf32,
    qs32,
    nsend,
    ssend,
    nrecv,
    srecv,
    att,
    a32,
    ysend,
    yrecv,
    ssem,
    rsem,
    lsem,
):
    me = lax.axis_index("seq")
    y = lax.axis_index("kv")
    c = lax.rem(me, CORES)
    chip = me // CORES
    other = 1 - c
    depth_chips = chips // ROW_CHIPS

    def load(src, dst, i):
        cp = pltpu.make_async_copy(src, dst, lsem.at[i])
        cp.start()
        return cp

    def remote(src, dst, i, seq, kv):
        return pltpu.make_async_remote_copy(
            src_ref=src,
            dst_ref=dst,
            send_sem=ssem.at[i],
            recv_sem=rsem.at[i],
            device_id={"kv": kv, "seq": seq},
            device_id_type=MESH,
        )

    load_q = load(q_hbm, qown, LQ)

    def far_first(k):
        a, b = k // ROW_CHIPS, lax.rem(k, ROW_CHIPS)
        return lax.rem(chip // ROW_CHIPS + far_offset(a, depth_chips), depth_chips) * ROW_CHIPS + far_in_row(b)

    def far_in_row(b):
        return lax.rem(chip + far_offset(b, ROW_CHIPS), ROW_CHIPS)

    def far_offset(k, size):
        step = jnp.where(lax.rem(k, 2) == 0, size // 2 - k // 2, size // 2 + (k + 1) // 2)
        return jnp.where(k == size - 1, 0, step)

    barrier = pltpu.get_barrier_semaphore()

    def greet(seq, kv):
        pl.semaphore_signal(barrier, inc=1, device_id={"kv": kv, "seq": seq}, device_id_type=MESH)

    def greet_plane(k, carry):
        greet(far_first(k) * CORES + c, y)
        return carry

    lax.fori_loop(0, chips - 1, greet_plane, 0, unroll=True)

    def greet_column(k, carry):
        kv = lax.rem(y + far_offset(k, groups), groups)
        greet(chip * CORES + c, kv)
        greet(chip * CORES + other, kv)
        return carry

    lax.fori_loop(0, groups - 1, greet_column, 0, unroll=True)
    greet(chip * CORES + other, y)

    load_o = load(os_hbm, osv, LO)
    load_ks = load(ks_hbm, ksv, LKS)
    load_vs = load(vs_hbm, vsv, LVS)
    load_k = load(k_hbm, kbuf.at[c], LK)
    load_v = load(v_hbm, vbuf.at[c], LV)
    load_w = load(w_hbm, wbuf.at[c], LW)
    load_sk = load(sk_hbm, skb, LSK)
    load_sv = load(sv_hbm, svb, LSV)
    load_sl = load(sl_hbm, sls, LSL)

    load_q.wait()
    for h in range(GROUP):
        piece = qown[:, h * WIDTH : (h + 1) * WIDTH].astype(F32)
        for s in range(OWN):
            q32[s * GROUP + h : s * GROUP + h + 1, :] = piece[s : s + 1, :]
    qg[c, chip] = q32[...].astype(BF16)

    pl.semaphore_wait(barrier, (chips - 1) + 2 * (groups - 1) + 1)

    def send_queries(k, carry):
        remote(qg.at[c, chip], qg.at[c, chip], SQ, far_first(k) * CORES + c, y).start()
        return carry

    lax.fori_loop(0, chips - 1, send_queries, 0, unroll=True)

    partner = chip * CORES + other
    swap_k = remote(k_hbm, kbuf.at[c], SK, partner, y)
    swap_k.start()
    swap_v = remote(v_hbm, vbuf.at[c], SV, partner, y)
    swap_v.start()
    swap_w = remote(w_hbm, wbuf.at[c], SW, partner, y)
    swap_w.start()
    load_ks.wait()
    load_vs.wait()
    blocks = ksv.shape[1]
    scb[c, 0:blocks, :] = jnp.concatenate(
        [jnp.broadcast_to(ksv[:, b : b + 1] * (WIDTH**-0.5 * LOG2E), (1, WIDTH)) for b in range(blocks)], axis=0
    )
    scb[c, blocks : 2 * blocks, :] = jnp.concatenate(
        [jnp.broadcast_to(vsv[:, b : b + 1], (1, WIDTH)) for b in range(blocks)], axis=0
    )
    swap_f = remote(scb.at[c], scb.at[c], SF, partner, y)
    swap_f.start()

    load_o.wait()
    samples = chips * CORES * OWN
    slots = chips * OWN
    s_i = lax.broadcasted_iota(jnp.int32, (samples, samples), 0)
    m_i = lax.broadcasted_iota(jnp.int32, (samples, samples), 1)
    m_in = lax.rem(m_i, slots)
    s_of_m = (m_in // OWN) * (CORES * OWN) + (m_i // slots) * OWN + lax.rem(m_i, OWN)
    spread = jnp.where(s_i == s_of_m, 1.0, 0.0).astype(BF16)
    owner_rows = jnp.broadcast_to(osv[...].astype(F32), (16, samples)).astype(BF16)
    owner = jnp.dot(owner_rows, spread, preferred_element_type=F32)[0:1, :]
    i_i = lax.broadcasted_iota(jnp.int32, (slots, samples), 0)
    slot_i = (i_i // OWN) * (CORES * OWN) + c * OWN + lax.rem(i_i, OWN)
    pick = jnp.where(owner == slot_i.astype(F32), 1.0, 0.0).astype(BF16)

    many_q = qg.at[0, pl.ds(0, chips - 1)]
    remote(many_q, many_q, SQ, partner, y).wait_recv()
    swap_q = remote(qg.at[c], qg.at[c], SC, partner, y)
    swap_q.start()
    swap_q.wait_recv()

    qf32[...] = qg[...].reshape(samples * GROUP, WIDTH).astype(F32)
    by_head = jnp.concatenate(
        [qf32[pl.ds(h, samples, stride=GROUP), :].astype(BF16) for h in range(GROUP)], axis=1
    )
    picked = jnp.dot(pick, by_head, preferred_element_type=F32)
    for h in range(GROUP):
        qs32[pl.ds(h, slots, stride=GROUP), :] = picked[:, h * WIDTH : (h + 1) * WIDTH]

    load_k.wait()
    load_v.wait()
    swap_k.wait_recv()
    swap_v.wait_recv()
    swap_f.wait_recv()

    chunk_chips = 8
    chunk = chunk_chips * ROWS
    chunks = chips // chunk_chips
    row_in = lax.rem(lax.broadcasted_iota(jnp.int32, (chunk, WIDTH), 0), ROWS)
    lane = lax.broadcasted_iota(jnp.int32, (chunk, WIDTH), 1)

    def prompt_chunk(n):
        first = pl.multiple_of(n * chunk, chunk)
        qc = qs32[pl.ds(first, chunk), :].astype(BF16)
        parts = []
        for core in range(CORES):
            s = nt_dot(qc, kbuf[core])
            for b in range(blocks):
                parts.append(s[:, b * SPAN : (b + 1) * SPAN] * scb[core, b : b + 1, :])
        peak = functools.reduce(jnp.maximum, parts)
        peak = jnp.max(peak, axis=1, keepdims=True)
        parts = [jnp.exp2(s - peak) for s in parts]
        total = jnp.sum(functools.reduce(jnp.add, parts), axis=1, keepdims=True)
        numer = None
        for core in range(CORES):
            scaled = jnp.concatenate(
                [
                    (parts[core * blocks + b] * scb[core, blocks + b : blocks + b + 1, :]).astype(BF16)
                    for b in range(blocks)
                ],
                axis=1,
            )
            term = jnp.dot(scaled, vbuf[core], preferred_element_type=F32)
            numer = term if numer is None else numer + term
        nsend[pl.ds(first, chunk), :] = numer.astype(BF16)
        stats = jnp.where(lane == row_in, peak, 0.0) + jnp.where(lane == row_in + ROWS, total, 0.0)
        stats = jnp.sum(stats.reshape(chunk_chips, ROWS, WIDTH), axis=1)
        for i in range(chunk_chips):
            ssend[n * chunk_chips + i] = stats[i : i + 1, :]

    def send_partial(t):
        first = pl.multiple_of(t * ROWS, ROWS)
        remote(ssend.at[t], srecv.at[chip], SS, t * CORES + c, y).start()
        remote(nsend.at[pl.ds(first, ROWS)], nrecv.at[chip], SN, t * CORES + c, y).start()

    own_chunk = chip // chunk_chips

    def chunk_step(k, carry):
        off = lax.rem(k + chunks // 2, chunks)
        n = lax.rem(own_chunk + off, chunks)
        prompt_chunk(n)

        def send_one(i, inner):
            t = n * chunk_chips + (i // ROW_CHIPS) * ROW_CHIPS + far_in_row(lax.rem(i, ROW_CHIPS))

            @pl.when(t != chip)
            def _():
                send_partial(t)

            return inner

        lax.fori_loop(0, chunk_chips, send_one, 0, unroll=True)
        return carry

    lax.fori_loop(0, chunks, chunk_step, 0)
    own_first = pl.multiple_of(chip * ROWS, ROWS)
    nrecv[chip] = nsend[pl.ds(own_first, ROWS), :]
    srecv[chip] = ssend[chip]

    load_sk.wait()
    load_sv.wait()
    load_sl.wait()
    own_q = qs32[pl.ds(own_first, ROWS), :].astype(BF16)
    limit = skb.shape[1]
    live_i = lax.broadcasted_iota(jnp.int32, (GROUP, limit), 1)
    near_numer, near_peak, near_total = [], [], []
    for j in range(OWN):
        live = live_i < sls[j]
        s = nt_dot(own_q, skb[j])[j * GROUP : (j + 1) * GROUP, :] * (WIDTH**-0.5 * LOG2E)
        s = jnp.where(live, s, NEG_FILL)
        peak = jnp.max(s, axis=1, keepdims=True)
        w = jnp.where(live, jnp.exp2(s - peak), 0.0)
        near_total.append(jnp.sum(w, axis=1, keepdims=True))
        near_peak.append(peak)
        w16 = jnp.concatenate([w, jnp.zeros_like(w)], axis=0).astype(BF16)
        near_numer.append(jnp.dot(w16, svb[j], preferred_element_type=F32)[:GROUP])
    near_numer = jnp.concatenate(near_numer, axis=0)
    near_peak = jnp.concatenate(near_peak, axis=0)
    near_total = jnp.concatenate(near_total, axis=0)

    many_s = srecv.at[pl.ds(0, chips - 1)]
    remote(many_s, many_s, SS, partner, y).wait_recv()
    stats = jnp.concatenate([srecv[i] for i in range(chips)], axis=0)
    stats = jnp.concatenate([stats, jnp.zeros((WIDTH - chips, WIDTH), F32)], axis=0)
    stats = jnp.transpose(stats)
    peaks = stats[0:ROWS, 0:chips]
    totals = stats[ROWS : 2 * ROWS, 0:chips]
    peak = jnp.maximum(jnp.max(peaks, axis=1, keepdims=True), near_peak)
    factor = jnp.exp2(peaks - peak)
    near_factor = jnp.exp2(near_peak - peak)
    total = jnp.sum(factor * totals, axis=1, keepdims=True) + near_total * near_factor
    many_n = nrecv.at[pl.ds(0, chips - 1)]
    remote(many_n, many_n, SN, partner, y).wait_recv()
    numer = near_numer * near_factor
    for i in range(chips):
        numer = numer + nrecv[i].astype(F32) * factor[:, i : i + 1]
    att[chip] = (numer / total).astype(BF16)

    def send_att(k, carry):
        remote(att.at[chip], att.at[chip], SA, far_first(k) * CORES + c, y).start()
        return carry

    lax.fori_loop(0, chips - 1, send_att, 0, unroll=True)
    load_w.wait()
    swap_w.wait_recv()
    many_a = att.at[pl.ds(0, chips - 1)]
    remote(many_a, many_a, SA, partner, y).wait_recv()

    a32[...] = att[...].reshape(slots * GROUP, WIDTH).astype(F32)
    rows = jnp.concatenate(
        [a32[pl.ds(h, slots, stride=GROUP), :].astype(BF16) for h in range(GROUP)], axis=1
    )
    per_group = slots // groups
    for core in range(CORES):
        part = nt_dot(rows, wbuf[core])
        ysend[core] = part.reshape(groups, per_group, part.shape[1])

    def send_out(k, carry):
        t = lax.rem(y + far_offset(k, groups), groups)
        remote(ysend.at[c, t], yrecv.at[c * groups + y], SY, chip * CORES + c, t).start()
        remote(ysend.at[other, t], yrecv.at[c * groups + y], SY, chip * CORES + other, t).start()
        return carry

    lax.fori_loop(0, groups - 1, send_out, 0, unroll=True)
    remote(ysend.at[other, y], yrecv.at[c * groups + y], SY, partner, y).start()
    yrecv[c * groups + y] = ysend[c, y]
    many_y = yrecv.at[pl.ds(0, CORES * groups - 1)]
    last = remote(many_y, many_y, SY, partner, y)
    last.wait_recv()
    for core in range(CORES):
        acc = yrecv[core * groups]
        for i in range(1, groups):
            acc = acc + yrecv[core * groups + i]
        for q in range(per_group // OWN):
            first = q * CORES * OWN + core * OWN
            o_ref[first : first + OWN, :] = acc[q * OWN : (q + 1) * OWN, :]

    remote(many_q, many_q, SQ, partner, y).wait_send()
    swap_q.wait_send()
    swap_k.wait_send()
    swap_v.wait_send()
    swap_w.wait_send()
    swap_f.wait_send()
    remote(many_s, many_s, SS, partner, y).wait_send()
    remote(many_n, many_n, SN, partner, y).wait_send()
    remote(many_a, many_a, SA, partner, y).wait_send()
    last.wait_send()


def local(
    queries,
    owner_slot,
    suffix_len,
    prompt_keys,
    prompt_value_rows,
    key_scale,
    value_block_scale,
    suffix_key_rows,
    suffix_value_rows,
    out_weight,
):
    groups = lax.axis_size("kv")
    chips = lax.axis_size("seq") // CORES
    samples = chips * CORES * OWN
    slots = chips * OWN
    positions = prompt_keys.shape[0]
    blocks = key_scale.shape[0]
    limit = suffix_key_rows.shape[1]
    depth, columns = out_weight.shape
    out_rows = samples // groups
    any_spec = pl.BlockSpec(memory_space=pl.ANY)
    return pl.pallas_call(
        functools.partial(kernel, chips, groups),
        out_shape=jax.ShapeDtypeStruct((out_rows, columns), F32),
        in_specs=[any_spec] * 10,
        out_specs=pl.BlockSpec(memory_space=pltpu.VMEM),
        scratch_shapes=[
            pltpu.VMEM(queries.shape, BF16),
            pltpu.VMEM((1, samples), jnp.int32),
            pltpu.SMEM((OWN,), jnp.int32),
            pltpu.VMEM((CORES, positions, WIDTH), BF16),
            pltpu.VMEM((CORES, positions, WIDTH), BF16),
            pltpu.VMEM((1, blocks), F32),
            pltpu.VMEM((1, blocks), F32),
            pltpu.VMEM((CORES, 2 * blocks, WIDTH), F32),
            pltpu.VMEM((OWN, limit, WIDTH), BF16),
            pltpu.VMEM((OWN, limit, WIDTH), BF16),
            pltpu.VMEM((CORES, columns, depth), BF16),
            pltpu.VMEM((ROWS, WIDTH), F32),
            pltpu.VMEM((CORES, chips, ROWS, WIDTH), BF16),
            pltpu.VMEM((samples * GROUP, WIDTH), F32),
            pltpu.VMEM((slots * GROUP, WIDTH), F32),
            pltpu.VMEM((slots * GROUP, WIDTH), BF16),
            pltpu.VMEM((chips, 1, WIDTH), F32),
            pltpu.VMEM((chips, ROWS, WIDTH), BF16),
            pltpu.VMEM((chips, 1, WIDTH), F32),
            pltpu.VMEM((chips, ROWS, WIDTH), BF16),
            pltpu.VMEM((slots * GROUP, WIDTH), F32),
            pltpu.VMEM((CORES, groups, slots // groups, columns), F32),
            pltpu.VMEM((CORES * groups, slots // groups, columns), F32),
            pltpu.SemaphoreType.DMA((10,)),
            pltpu.SemaphoreType.DMA((10,)),
            pltpu.SemaphoreType.DMA((10,)),
        ],
        compiler_params=pltpu.CompilerParams(
            collective_id=0, has_side_effects=True, vmem_limit_bytes=56508416
        ),
        name="decode_attention",
    )(
        queries,
        owner_slot.reshape(1, samples),
        suffix_len,
        prompt_keys,
        prompt_value_rows,
        key_scale.reshape(1, blocks),
        value_block_scale.reshape(1, blocks),
        suffix_key_rows,
        suffix_value_rows,
        out_weight.T,
    )


def solution(mesh):
    in_specs = (
        P("seq", "kv"),
        P(),
        P("seq"),
        P("seq", "kv"),
        P("seq", "kv"),
        P("seq", "kv"),
        P("seq", "kv"),
        P("seq", None, "kv"),
        P("seq", None, "kv"),
        P("kv", "seq"),
    )
    out_specs = P("kv", "seq")
    return jax.shard_map(local, mesh=mesh, in_specs=in_specs, out_specs=out_specs, check_vma=False)
```

```python
import functools

import jax
import jax.numpy as jnp
from jax import lax
from jax.experimental import pallas as pl
from jax.experimental.pallas import tpu as pltpu
from jax.sharding import PartitionSpec as P

MESH = pl.DeviceIdType.MESH
F32 = jnp.float32
BF16 = jnp.bfloat16
LOG2E = 1.4426950408889634
NEG_FILL = -1e30

CORES = 2
ROW_CHIPS = 4
GROUP = 8
WIDTH = 128
OWN = 2
ROWS = OWN * GROUP
SPAN = 128

SQ, SC, SK, SV, SW, SF, SN, SS, SA, SY = range(10)
LQ, LO, LK, LV, LKS, LVS, LW, LSK, LSV, LSL = range(10)


def nt_dot(a, b):
    return lax.dot_general(a, b, (((1,), (1,)), ((), ())), preferred_element_type=F32)


def kernel(
    chips,
    groups,
    q_hbm,
    os_hbm,
    sl_hbm,
    k_hbm,
    v_hbm,
    ks_hbm,
    vs_hbm,
    sk_hbm,
    sv_hbm,
    w_hbm,
    o_ref,
    qown,
    osv,
    sls,
    kbuf,
    vbuf,
    ksv,
    vsv,
    scb,
    skb,
    svb,
    wbuf,
    q32,
    qg,
    qf32,
    qs32,
    nsend,
    ssend,
    nrecv,
    srecv,
    att,
    a32,
    ysend,
    yrecv,
    ssem,
    rsem,
    lsem,
):
    me = lax.axis_index("seq")
    y = lax.axis_index("kv")
    c = lax.rem(me, CORES)
    chip = me // CORES
    other = 1 - c
    depth_chips = chips // ROW_CHIPS

    def load(src, dst, i):
        cp = pltpu.make_async_copy(src, dst, lsem.at[i])
        cp.start()
        return cp

    def remote(src, dst, i, seq, kv):
        return pltpu.make_async_remote_copy(
            src_ref=src,
            dst_ref=dst,
            send_sem=ssem.at[i],
            recv_sem=rsem.at[i],
            device_id={"kv": kv, "seq": seq},
            device_id_type=MESH,
        )

    load_q = load(q_hbm, qown, LQ)

    def far_first(k):
        a, b = k // ROW_CHIPS, lax.rem(k, ROW_CHIPS)
        return lax.rem(chip // ROW_CHIPS + far_offset(a, depth_chips), depth_chips) * ROW_CHIPS + far_in_row(b)

    def far_in_row(b):
        return lax.rem(chip + far_offset(b, ROW_CHIPS), ROW_CHIPS)

    def far_offset(k, size):
        step = jnp.where(lax.rem(k, 2) == 0, size // 2 - k // 2, size // 2 + (k + 1) // 2)
        return jnp.where(k == size - 1, 0, step)

    barrier = pltpu.get_barrier_semaphore()

    def greet(seq, kv):
        pl.semaphore_signal(barrier, inc=1, device_id={"kv": kv, "seq": seq}, device_id_type=MESH)

    def greet_plane(k, carry):
        greet(far_first(k) * CORES + c, y)
        return carry

    lax.fori_loop(0, chips - 1, greet_plane, 0, unroll=True)

    def greet_column(k, carry):
        kv = lax.rem(y + far_offset(k, groups), groups)
        greet(chip * CORES + c, kv)
        greet(chip * CORES + other, kv)
        return carry

    lax.fori_loop(0, groups - 1, greet_column, 0, unroll=True)
    greet(chip * CORES + other, y)

    load_o = load(os_hbm, osv, LO)
    load_ks = load(ks_hbm, ksv, LKS)
    load_vs = load(vs_hbm, vsv, LVS)
    load_k = load(k_hbm, kbuf.at[c], LK)
    load_v = load(v_hbm, vbuf.at[c], LV)
    load_w = load(w_hbm, wbuf.at[c], LW)
    load_sk = load(sk_hbm, skb, LSK)
    load_sv = load(sv_hbm, svb, LSV)
    load_sl = load(sl_hbm, sls, LSL)

    load_q.wait()
    for h in range(GROUP):
        piece = qown[:, h * WIDTH : (h + 1) * WIDTH].astype(F32)
        for s in range(OWN):
            q32[s * GROUP + h : s * GROUP + h + 1, :] = piece[s : s + 1, :]
    qg[c, chip] = q32[...].astype(BF16)

    pl.semaphore_wait(barrier, (chips - 1) + 2 * (groups - 1) + 1)

    def send_queries(k, carry):
        remote(qg.at[c, chip], qg.at[c, chip], SQ, far_first(k) * CORES + c, y).start()
        return carry

    lax.fori_loop(0, chips - 1, send_queries, 0, unroll=True)

    partner = chip * CORES + other
    swap_k = remote(k_hbm, kbuf.at[c], SK, partner, y)
    swap_k.start()
    swap_v = remote(v_hbm, vbuf.at[c], SV, partner, y)
    swap_v.start()
    swap_w = remote(w_hbm, wbuf.at[c], SW, partner, y)
    swap_w.start()
    load_ks.wait()
    load_vs.wait()
    blocks = ksv.shape[1]
    scb[c, 0:blocks, :] = jnp.concatenate(
        [jnp.broadcast_to(ksv[:, b : b + 1] * (WIDTH**-0.5 * LOG2E), (1, WIDTH)) for b in range(blocks)], axis=0
    )
    scb[c, blocks : 2 * blocks, :] = jnp.concatenate(
        [jnp.broadcast_to(vsv[:, b : b + 1], (1, WIDTH)) for b in range(blocks)], axis=0
    )
    swap_f = remote(scb.at[c], scb.at[c], SF, partner, y)
    swap_f.start()

    load_o.wait()
    samples = chips * CORES * OWN
    slots = chips * OWN
    s_i = lax.broadcasted_iota(jnp.int32, (samples, samples), 0)
    m_i = lax.broadcasted_iota(jnp.int32, (samples, samples), 1)
    m_in = lax.rem(m_i, slots)
    s_of_m = (m_in // OWN) * (CORES * OWN) + (m_i // slots) * OWN + lax.rem(m_i, OWN)
    spread = jnp.where(s_i == s_of_m, 1.0, 0.0).astype(BF16)
    owner_rows = jnp.broadcast_to(osv[...].astype(F32), (16, samples)).astype(BF16)
    owner = jnp.dot(owner_rows, spread, preferred_element_type=F32)[0:1, :]
    i_i = lax.broadcasted_iota(jnp.int32, (slots, samples), 0)
    slot_i = (i_i // OWN) * (CORES * OWN) + c * OWN + lax.rem(i_i, OWN)
    pick = jnp.where(owner == slot_i.astype(F32), 1.0, 0.0).astype(BF16)

    many_q = qg.at[0, pl.ds(0, chips - 1)]
    remote(many_q, many_q, SQ, partner, y).wait_recv()
    swap_q = remote(qg.at[c], qg.at[c], SC, partner, y)
    swap_q.start()
    swap_q.wait_recv()

    qf32[...] = qg[...].reshape(samples * GROUP, WIDTH).astype(F32)
    by_head = jnp.concatenate(
        [qf32[pl.ds(h, samples, stride=GROUP), :].astype(BF16) for h in range(GROUP)], axis=1
    )
    picked = jnp.dot(pick, by_head, preferred_element_type=F32)
    for h in range(GROUP):
        qs32[pl.ds(h, slots, stride=GROUP), :] = picked[:, h * WIDTH : (h + 1) * WIDTH]

    load_k.wait()
    load_v.wait()
    swap_k.wait_recv()
    swap_v.wait_recv()
    swap_f.wait_recv()

    chunk_chips = 8
    chunk = chunk_chips * ROWS
    chunks = chips // chunk_chips
    row_in = lax.rem(lax.broadcasted_iota(jnp.int32, (chunk, WIDTH), 0), ROWS)
    lane = lax.broadcasted_iota(jnp.int32, (chunk, WIDTH), 1)

    def prompt_chunk(n):
        first = pl.multiple_of(n * chunk, chunk)
        qc = qs32[pl.ds(first, chunk), :].astype(BF16)
        parts = []
        for core in range(CORES):
            s = nt_dot(qc, kbuf[core])
            for b in range(blocks):
                parts.append(s[:, b * SPAN : (b + 1) * SPAN] * scb[core, b : b + 1, :])
        peak = functools.reduce(jnp.maximum, parts)
        peak = jnp.max(peak, axis=1, keepdims=True)
        parts = [jnp.exp2(s - peak) for s in parts]
        total = jnp.sum(functools.reduce(jnp.add, parts), axis=1, keepdims=True)
        numer = None
        for core in range(CORES):
            scaled = jnp.concatenate(
                [
                    (parts[core * blocks + b] * scb[core, blocks + b : blocks + b + 1, :]).astype(BF16)
                    for b in range(blocks)
                ],
                axis=1,
            )
            term = jnp.dot(scaled, vbuf[core], preferred_element_type=F32)
            numer = term if numer is None else numer + term
        nsend[pl.ds(first, chunk), :] = numer.astype(BF16)
        stats = jnp.where(lane == row_in, peak, 0.0) + jnp.where(lane == row_in + ROWS, total, 0.0)
        stats = jnp.sum(stats.reshape(chunk_chips, ROWS, WIDTH), axis=1)
        for i in range(chunk_chips):
            ssend[n * chunk_chips + i] = stats[i : i + 1, :]

    def send_partial(t):
        first = pl.multiple_of(t * ROWS, ROWS)
        remote(ssend.at[t], srecv.at[chip], SS, t * CORES + c, y).start()
        remote(nsend.at[pl.ds(first, ROWS)], nrecv.at[chip], SN, t * CORES + c, y).start()

    own_chunk = chip // chunk_chips

    def chunk_step(k, carry):
        off = lax.rem(k + chunks // 2, chunks)
        n = lax.rem(own_chunk + off, chunks)
        prompt_chunk(n)

        def send_one(i, inner):
            t = n * chunk_chips + (i // ROW_CHIPS) * ROW_CHIPS + far_in_row(lax.rem(i, ROW_CHIPS))

            @pl.when(t != chip)
            def _():
                send_partial(t)

            return inner

        lax.fori_loop(0, chunk_chips, send_one, 0, unroll=True)
        return carry

    lax.fori_loop(0, chunks, chunk_step, 0)
    own_first = pl.multiple_of(chip * ROWS, ROWS)
    nrecv[chip] = nsend[pl.ds(own_first, ROWS), :]
    srecv[chip] = ssend[chip]

    load_sk.wait()
    load_sv.wait()
    load_sl.wait()
    own_q = qs32[pl.ds(own_first, ROWS), :].astype(BF16)
    limit = skb.shape[1]
    live_i = lax.broadcasted_iota(jnp.int32, (GROUP, limit), 1)
    near_numer, near_peak, near_total = [], [], []
    for j in range(OWN):
        live = live_i < sls[j]
        s = nt_dot(own_q, skb[j])[j * GROUP : (j + 1) * GROUP, :] * (WIDTH**-0.5 * LOG2E)
        s = jnp.where(live, s, NEG_FILL)
        peak = jnp.max(s, axis=1, keepdims=True)
        w = jnp.where(live, jnp.exp2(s - peak), 0.0)
        near_total.append(jnp.sum(w, axis=1, keepdims=True))
        near_peak.append(peak)
        w16 = jnp.concatenate([w, jnp.zeros_like(w)], axis=0).astype(BF16)
        near_numer.append(jnp.dot(w16, svb[j], preferred_element_type=F32)[:GROUP])
    near_numer = jnp.concatenate(near_numer, axis=0)
    near_peak = jnp.concatenate(near_peak, axis=0)
    near_total = jnp.concatenate(near_total, axis=0)

    many_s = srecv.at[pl.ds(0, chips - 1)]
    remote(many_s, many_s, SS, partner, y).wait_recv()
    stats = jnp.concatenate([srecv[i] for i in range(chips)], axis=0)
    stats = jnp.concatenate([stats, jnp.zeros((WIDTH - chips, WIDTH), F32)], axis=0)
    stats = jnp.transpose(stats)
    peaks = stats[0:ROWS, 0:chips]
    totals = stats[ROWS : 2 * ROWS, 0:chips]
    peak = jnp.maximum(jnp.max(peaks, axis=1, keepdims=True), near_peak)
    factor = jnp.exp2(peaks - peak)
    near_factor = jnp.exp2(near_peak - peak)
    total = jnp.sum(factor * totals, axis=1, keepdims=True) + near_total * near_factor
    many_n = nrecv.at[pl.ds(0, chips - 1)]
    remote(many_n, many_n, SN, partner, y).wait_recv()
    numer = near_numer * near_factor
    for i in range(chips):
        numer = numer + nrecv[i].astype(F32) * factor[:, i : i + 1]
    att[chip] = (numer / total).astype(BF16)

    def send_att(k, carry):
        remote(att.at[chip], att.at[chip], SA, far_first(k) * CORES + c, y).start()
        return carry

    lax.fori_loop(0, chips - 1, send_att, 0, unroll=True)
    load_w.wait()
    swap_w.wait_recv()
    many_a = att.at[pl.ds(0, chips - 1)]
    remote(many_a, many_a, SA, partner, y).wait_recv()

    a32[...] = att[...].reshape(slots * GROUP, WIDTH).astype(F32)
    rows = jnp.concatenate(
        [a32[pl.ds(h, slots, stride=GROUP), :].astype(BF16) for h in range(GROUP)], axis=1
    )
    per_group = slots // groups
    for core in range(CORES):
        part = nt_dot(rows, wbuf[core])
        ysend[core] = part.reshape(groups, per_group, part.shape[1])

    def send_out(k, carry):
        t = lax.rem(y + far_offset(k, groups), groups)
        remote(ysend.at[c, t], yrecv.at[c * groups + y], SY, chip * CORES + c, t).start()
        remote(ysend.at[other, t], yrecv.at[c * groups + y], SY, chip * CORES + other, t).start()
        return carry

    lax.fori_loop(0, groups - 1, send_out, 0, unroll=True)
    remote(ysend.at[other, y], yrecv.at[c * groups + y], SY, partner, y).start()
    yrecv[c * groups + y] = ysend[c, y]
    many_y = yrecv.at[pl.ds(0, CORES * groups - 1)]
    last = remote(many_y, many_y, SY, partner, y)
    last.wait_recv()
    for core in range(CORES):
        acc = yrecv[core * groups]
        for i in range(1, groups):
            acc = acc + yrecv[core * groups + i]
        for q in range(per_group // OWN):
            first = q * CORES * OWN + core * OWN
            o_ref[first : first + OWN, :] = acc[q * OWN : (q + 1) * OWN, :]

    remote(many_q, many_q, SQ, partner, y).wait_send()
    swap_q.wait_send()
    swap_k.wait_send()
    swap_v.wait_send()
    swap_w.wait_send()
    swap_f.wait_send()
    remote(many_s, many_s, SS, partner, y).wait_send()
    remote(many_n, many_n, SN, partner, y).wait_send()
    remote(many_a, many_a, SA, partner, y).wait_send()
    last.wait_send()


def local(
    queries,
    owner_slot,
    suffix_len,
    prompt_keys,
    prompt_value_rows,
    key_scale,
    value_block_scale,
    suffix_key_rows,
    suffix_value_rows,
    out_weight,
):
    groups = lax.axis_size("kv")
    chips = lax.axis_size("seq") // CORES
    samples = chips * CORES * OWN
    slots = chips * OWN
    positions = prompt_keys.shape[0]
    blocks = key_scale.shape[0]
    limit = suffix_key_rows.shape[1]
    depth, columns = out_weight.shape
    out_rows = samples // groups
    any_spec = pl.BlockSpec(memory_space=pl.ANY)
    return pl.pallas_call(
        functools.partial(kernel, chips, groups),
        out_shape=pltpu.VMEM((out_rows, columns), F32),
        in_specs=[any_spec] * 10,
        out_specs=pl.BlockSpec(memory_space=pltpu.VMEM),
        scratch_shapes=[
            pltpu.VMEM(queries.shape, BF16),
            pltpu.VMEM((1, samples), jnp.int32),
            pltpu.SMEM((OWN,), jnp.int32),
            pltpu.VMEM((CORES, positions, WIDTH), BF16),
            pltpu.VMEM((CORES, positions, WIDTH), BF16),
            pltpu.VMEM((1, blocks), F32),
            pltpu.VMEM((1, blocks), F32),
            pltpu.VMEM((CORES, 2 * blocks, WIDTH), F32),
            pltpu.VMEM((OWN, limit, WIDTH), BF16),
            pltpu.VMEM((OWN, limit, WIDTH), BF16),
            pltpu.VMEM((CORES, columns, depth), BF16),
            pltpu.VMEM((ROWS, WIDTH), F32),
            pltpu.VMEM((CORES, chips, ROWS, WIDTH), BF16),
            pltpu.VMEM((samples * GROUP, WIDTH), F32),
            pltpu.VMEM((slots * GROUP, WIDTH), F32),
            pltpu.VMEM((slots * GROUP, WIDTH), BF16),
            pltpu.VMEM((chips, 1, WIDTH), F32),
            pltpu.VMEM((chips, ROWS, WIDTH), BF16),
            pltpu.VMEM((chips, 1, WIDTH), F32),
            pltpu.VMEM((chips, ROWS, WIDTH), BF16),
            pltpu.VMEM((slots * GROUP, WIDTH), F32),
            pltpu.VMEM((CORES, groups, slots // groups, columns), F32),
            pltpu.VMEM((CORES * groups, slots // groups, columns), F32),
            pltpu.SemaphoreType.DMA((10,)),
            pltpu.SemaphoreType.DMA((10,)),
            pltpu.SemaphoreType.DMA((10,)),
        ],
        compiler_params=pltpu.CompilerParams(
            collective_id=0, has_side_effects=True, vmem_limit_bytes=60 * 1024 * 1024
        ),
        name="decode_attention",
    )(
        queries,
        owner_slot.reshape(1, samples),
        suffix_len,
        prompt_keys,
        prompt_value_rows,
        key_scale.reshape(1, blocks),
        value_block_scale.reshape(1, blocks),
        suffix_key_rows,
        suffix_value_rows,
        out_weight.T,
    )


def solution(mesh):
    in_specs = (
        P("seq", "kv"),
        P(),
        P("seq"),
        P("seq", "kv"),
        P("seq", "kv"),
        P("seq", "kv"),
        P("seq", "kv"),
        P("seq", None, "kv"),
        P("seq", None, "kv"),
        P("kv", "seq"),
    )
    out_specs = P("kv", "seq")
    return jax.shard_map(local, mesh=mesh, in_specs=in_specs, out_specs=out_specs, check_vma=False)
```

```python
import functools

import jax
import jax.numpy as jnp
from jax import lax
from jax.experimental import pallas as pl
from jax.experimental.pallas import tpu as pltpu
from jax.sharding import PartitionSpec as P

MESH = pl.DeviceIdType.MESH
F32 = jnp.float32
BF16 = jnp.bfloat16
LOG2E = 1.4426950408889634
NEG_FILL = -1e30

CORES = 2
ROW_CHIPS = 4
GROUP = 8
WIDTH = 128
OWN = 2
ROWS = OWN * GROUP
SPAN = 128

SQ, SC, SK, SV, SW, SF, SN, SS, SA, SY = range(10)
LQ, LO, LK, LV, LKS, LVS, LW, LSK, LSV, LSL = range(10)


def nt_dot(a, b):
    return lax.dot_general(a, b, (((1,), (1,)), ((), ())), preferred_element_type=F32)


def near_first(size):
    return [0] + [k for step in range(1, size // 2) for k in (step, size - step)] + [size // 2]


def kernel(
    chips,
    groups,
    q_hbm,
    os_hbm,
    sl_hbm,
    k_hbm,
    v_hbm,
    ks_hbm,
    vs_hbm,
    sk_hbm,
    sv_hbm,
    w_hbm,
    o_ref,
    qown,
    osv,
    sls,
    kbuf,
    vbuf,
    ksv,
    vsv,
    scb,
    skb,
    svb,
    wbuf,
    q32,
    qg,
    qf32,
    qs32,
    nsend,
    ssend,
    nrecv,
    srecv,
    att,
    a32,
    ysend,
    yrecv,
    ssem,
    rsem,
    lsem,
    asem,
):
    me = lax.axis_index("seq")
    y = lax.axis_index("kv")
    c = lax.rem(me, CORES)
    chip = me // CORES
    other = 1 - c
    depth_chips = chips // ROW_CHIPS

    def load(src, dst, i):
        cp = pltpu.make_async_copy(src, dst, lsem.at[i])
        cp.start()
        return cp

    def remote(src, dst, i, seq, kv):
        return pltpu.make_async_remote_copy(
            src_ref=src,
            dst_ref=dst,
            send_sem=ssem.at[i],
            recv_sem=rsem.at[i],
            device_id={"kv": kv, "seq": seq},
            device_id_type=MESH,
        )

    load_q = load(q_hbm, qown, LQ)

    def far_first(k):
        a, b = k // ROW_CHIPS, lax.rem(k, ROW_CHIPS)
        return lax.rem(chip // ROW_CHIPS + far_offset(a, depth_chips), depth_chips) * ROW_CHIPS + far_in_row(b)

    def far_in_row(b):
        return lax.rem(chip + far_offset(b, ROW_CHIPS), ROW_CHIPS)

    def far_offset(k, size):
        step = jnp.where(lax.rem(k, 2) == 0, size // 2 - k // 2, size // 2 + (k + 1) // 2)
        return jnp.where(k == size - 1, 0, step)

    barrier = pltpu.get_barrier_semaphore()

    def greet(seq, kv):
        pl.semaphore_signal(barrier, inc=1, device_id={"kv": kv, "seq": seq}, device_id_type=MESH)

    def greet_plane(k, carry):
        greet(far_first(k) * CORES + c, y)
        return carry

    lax.fori_loop(0, chips - 1, greet_plane, 0, unroll=True)

    def greet_column(k, carry):
        kv = lax.rem(y + far_offset(k, groups), groups)
        greet(chip * CORES + c, kv)
        greet(chip * CORES + other, kv)
        return carry

    lax.fori_loop(0, groups - 1, greet_column, 0, unroll=True)
    greet(chip * CORES + other, y)

    load_o = load(os_hbm, osv, LO)
    load_ks = load(ks_hbm, ksv, LKS)
    load_vs = load(vs_hbm, vsv, LVS)
    load_k = load(k_hbm, kbuf.at[c], LK)
    load_v = load(v_hbm, vbuf.at[c], LV)
    load_w = load(w_hbm, wbuf.at[c], LW)
    load_sk = load(sk_hbm, skb, LSK)
    load_sv = load(sv_hbm, svb, LSV)
    load_sl = load(sl_hbm, sls, LSL)

    load_q.wait()
    for h in range(GROUP):
        piece = qown[:, h * WIDTH : (h + 1) * WIDTH].astype(F32)
        for s in range(OWN):
            q32[s * GROUP + h : s * GROUP + h + 1, :] = piece[s : s + 1, :]
    qg[c, chip] = q32[...].astype(BF16)

    pl.semaphore_wait(barrier, (chips - 1) + 2 * (groups - 1) + 1)

    def send_queries(k, carry):
        remote(qg.at[c, chip], qg.at[c, chip], SQ, far_first(k) * CORES + c, y).start()
        return carry

    lax.fori_loop(0, chips - 1, send_queries, 0, unroll=True)

    partner = chip * CORES + other
    swap_k = remote(k_hbm, kbuf.at[c], SK, partner, y)
    swap_k.start()
    swap_v = remote(v_hbm, vbuf.at[c], SV, partner, y)
    swap_v.start()
    swap_w = remote(w_hbm, wbuf.at[c], SW, partner, y)
    swap_w.start()
    load_ks.wait()
    load_vs.wait()
    blocks = ksv.shape[1]
    scb[c, 0:blocks, :] = jnp.concatenate(
        [jnp.broadcast_to(ksv[:, b : b + 1] * (WIDTH**-0.5 * LOG2E), (1, WIDTH)) for b in range(blocks)], axis=0
    )
    scb[c, blocks : 2 * blocks, :] = jnp.concatenate(
        [jnp.broadcast_to(vsv[:, b : b + 1], (1, WIDTH)) for b in range(blocks)], axis=0
    )
    swap_f = remote(scb.at[c], scb.at[c], SF, partner, y)
    swap_f.start()

    load_o.wait()
    samples = chips * CORES * OWN
    slots = chips * OWN
    s_i = lax.broadcasted_iota(jnp.int32, (samples, samples), 0)
    m_i = lax.broadcasted_iota(jnp.int32, (samples, samples), 1)
    m_in = lax.rem(m_i, slots)
    s_of_m = (m_in // OWN) * (CORES * OWN) + (m_i // slots) * OWN + lax.rem(m_i, OWN)
    spread = jnp.where(s_i == s_of_m, 1.0, 0.0).astype(BF16)
    owner_rows = jnp.broadcast_to(osv[...].astype(F32), (16, samples)).astype(BF16)
    owner = jnp.dot(owner_rows, spread, preferred_element_type=F32)[0:1, :]
    i_i = lax.broadcasted_iota(jnp.int32, (slots, samples), 0)
    slot_i = (i_i // OWN) * (CORES * OWN) + c * OWN + lax.rem(i_i, OWN)
    pick = jnp.where(owner == slot_i.astype(F32), 1.0, 0.0).astype(BF16)

    many_q = qg.at[0, pl.ds(0, chips - 1)]
    remote(many_q, many_q, SQ, partner, y).wait_recv()
    swap_q = remote(qg.at[c], qg.at[c], SC, partner, y)
    swap_q.start()
    swap_q.wait_recv()

    qf32[...] = qg[...].reshape(samples * GROUP, WIDTH).astype(F32)
    by_head = jnp.concatenate(
        [qf32[pl.ds(h, samples, stride=GROUP), :].astype(BF16) for h in range(GROUP)], axis=1
    )
    picked = jnp.dot(pick, by_head, preferred_element_type=F32)
    for h in range(GROUP):
        qs32[pl.ds(h, slots, stride=GROUP), :] = picked[:, h * WIDTH : (h + 1) * WIDTH]

    load_k.wait()
    load_v.wait()
    swap_k.wait_recv()
    swap_v.wait_recv()
    swap_f.wait_recv()

    chunk_chips = 8
    chunk = chunk_chips * ROWS
    chunks = chips // chunk_chips
    row_in = lax.rem(lax.broadcasted_iota(jnp.int32, (chunk, WIDTH), 0), ROWS)
    lane = lax.broadcasted_iota(jnp.int32, (chunk, WIDTH), 1)

    def prompt_chunk(n):
        first = pl.multiple_of(n * chunk, chunk)
        qc = qs32[pl.ds(first, chunk), :].astype(BF16)
        parts = []
        for core in range(CORES):
            s = nt_dot(qc, kbuf[core])
            for b in range(blocks):
                parts.append(s[:, b * SPAN : (b + 1) * SPAN] * scb[core, b : b + 1, :])
        peak = functools.reduce(jnp.maximum, parts)
        peak = jnp.max(peak, axis=1, keepdims=True)
        parts = [jnp.exp2(s - peak) for s in parts]
        total = jnp.sum(functools.reduce(jnp.add, parts), axis=1, keepdims=True)
        numer = None
        for core in range(CORES):
            scaled = jnp.concatenate(
                [
                    (parts[core * blocks + b] * scb[core, blocks + b : blocks + b + 1, :]).astype(BF16)
                    for b in range(blocks)
                ],
                axis=1,
            )
            term = jnp.dot(scaled, vbuf[core], preferred_element_type=F32)
            numer = term if numer is None else numer + term
        nsend[pl.ds(first, chunk), :] = numer.astype(BF16)
        stats = jnp.where(lane == row_in, peak, 0.0) + jnp.where(lane == row_in + ROWS, total, 0.0)
        stats = jnp.sum(stats.reshape(chunk_chips, ROWS, WIDTH), axis=1)
        for i in range(chunk_chips):
            ssend[n * chunk_chips + i] = stats[i : i + 1, :]

    def send_partial(t):
        first = pl.multiple_of(t * ROWS, ROWS)
        remote(ssend.at[t], srecv.at[chip], SS, t * CORES + c, y).start()
        remote(nsend.at[pl.ds(first, ROWS)], nrecv.at[chip], SN, t * CORES + c, y).start()

    own_chunk = chip // chunk_chips

    def chunk_step(k, carry):
        off = lax.rem(k + chunks // 2, chunks)
        n = lax.rem(own_chunk + off, chunks)
        prompt_chunk(n)

        def send_one(i, inner):
            t = n * chunk_chips + (i // ROW_CHIPS) * ROW_CHIPS + far_in_row(lax.rem(i, ROW_CHIPS))

            @pl.when(t != chip)
            def _():
                send_partial(t)

            return inner

        lax.fori_loop(0, chunk_chips, send_one, 0, unroll=True)
        return carry

    lax.fori_loop(0, chunks, chunk_step, 0)
    own_first = pl.multiple_of(chip * ROWS, ROWS)
    nrecv[chip] = nsend[pl.ds(own_first, ROWS), :]
    srecv[chip] = ssend[chip]

    load_sk.wait()
    load_sv.wait()
    load_sl.wait()
    own_q = qs32[pl.ds(own_first, ROWS), :].astype(BF16)
    limit = skb.shape[1]
    live_i = lax.broadcasted_iota(jnp.int32, (GROUP, limit), 1)
    near_numer, near_peak, near_total = [], [], []
    for j in range(OWN):
        live = live_i < sls[j]
        s = nt_dot(own_q, skb[j])[j * GROUP : (j + 1) * GROUP, :] * (WIDTH**-0.5 * LOG2E)
        s = jnp.where(live, s, NEG_FILL)
        peak = jnp.max(s, axis=1, keepdims=True)
        w = jnp.where(live, jnp.exp2(s - peak), 0.0)
        near_total.append(jnp.sum(w, axis=1, keepdims=True))
        near_peak.append(peak)
        w16 = jnp.concatenate([w, jnp.zeros_like(w)], axis=0).astype(BF16)
        near_numer.append(jnp.dot(w16, svb[j], preferred_element_type=F32)[:GROUP])
    near_numer = jnp.concatenate(near_numer, axis=0)
    near_peak = jnp.concatenate(near_peak, axis=0)
    near_total = jnp.concatenate(near_total, axis=0)

    many_s = srecv.at[pl.ds(0, chips - 1)]
    remote(many_s, many_s, SS, partner, y).wait_recv()
    stats = jnp.concatenate([srecv[i] for i in range(chips)], axis=0)
    stats = jnp.concatenate([stats, jnp.zeros((WIDTH - chips, WIDTH), F32)], axis=0)
    stats = jnp.transpose(stats)
    peaks = stats[0:ROWS, 0:chips]
    totals = stats[ROWS : 2 * ROWS, 0:chips]
    peak = jnp.maximum(jnp.max(peaks, axis=1, keepdims=True), near_peak)
    factor = jnp.exp2(peaks - peak)
    near_factor = jnp.exp2(near_peak - peak)
    total = jnp.sum(factor * totals, axis=1, keepdims=True) + near_total * near_factor
    many_n = nrecv.at[pl.ds(0, chips - 1)]
    remote(many_n, many_n, SN, partner, y).wait_recv()
    numer = near_numer * near_factor
    for i in range(chips):
        numer = numer + nrecv[i].astype(F32) * factor[:, i : i + 1]
    att[chip] = (numer / total).astype(BF16)

    def send_att(k, carry):
        pltpu.make_async_remote_copy(
            src_ref=att.at[chip],
            dst_ref=att.at[chip],
            send_sem=ssem.at[SA],
            recv_sem=asem.at[far_offset(k // ROW_CHIPS, depth_chips)],
            device_id={"kv": y, "seq": far_first(k) * CORES + c},
            device_id_type=MESH,
        ).start()
        return carry

    lax.fori_loop(0, chips - 1, send_att, 0, unroll=True)
    load_w.wait()
    swap_w.wait_recv()
    row = chip // ROW_CHIPS
    per_group = ROW_CHIPS * OWN
    for n, k in enumerate(near_first(depth_chips)):
        t = lax.rem(row + depth_chips - k, depth_chips)
        arrived = att.at[pl.ds(0, ROW_CHIPS - (k == 0))]
        pltpu.make_async_remote_copy(
            src_ref=arrived,
            dst_ref=arrived,
            send_sem=ssem.at[SA],
            recv_sem=asem.at[k],
            device_id={"kv": y, "seq": partner},
            device_id_type=MESH,
        ).wait_recv()
        first = pl.multiple_of(t * ROW_CHIPS, ROW_CHIPS)
        a32[n] = att[pl.ds(first, ROW_CHIPS)].reshape(per_group * GROUP, WIDTH).astype(F32)
        rows = jnp.concatenate(
            [a32[n, pl.ds(h, per_group, stride=GROUP), :].astype(BF16) for h in range(GROUP)], axis=1
        )
        for core in range(CORES):
            ysend[core, n] = nt_dot(rows, wbuf[core])
        remote(ysend.at[other, n], yrecv.at[c * groups + y], SY, chip * CORES + other, t).start()

        @pl.when(t != y)
        def _():
            remote(ysend.at[c, n], yrecv.at[c * groups + y], SY, chip * CORES + c, t).start()

        @pl.when(t == y)
        def _():
            yrecv[c * groups + y] = ysend[c, n]

    many_y = yrecv.at[pl.ds(0, CORES * groups - 1)]
    last = remote(many_y, many_y, SY, partner, y)
    last.wait_recv()
    for core in range(CORES):
        acc = yrecv[core * groups]
        for i in range(1, groups):
            acc = acc + yrecv[core * groups + i]
        for q in range(per_group // OWN):
            first = q * CORES * OWN + core * OWN
            o_ref[first : first + OWN, :] = acc[q * OWN : (q + 1) * OWN, :]

    remote(many_q, many_q, SQ, partner, y).wait_send()
    swap_q.wait_send()
    swap_k.wait_send()
    swap_v.wait_send()
    swap_w.wait_send()
    swap_f.wait_send()
    remote(many_s, many_s, SS, partner, y).wait_send()
    remote(many_n, many_n, SN, partner, y).wait_send()
    many_a = att.at[pl.ds(0, chips - 1)]
    remote(many_a, many_a, SA, partner, y).wait_send()
    last.wait_send()


def local(
    queries,
    owner_slot,
    suffix_len,
    prompt_keys,
    prompt_value_rows,
    key_scale,
    value_block_scale,
    suffix_key_rows,
    suffix_value_rows,
    out_weight,
):
    groups = lax.axis_size("kv")
    chips = lax.axis_size("seq") // CORES
    samples = chips * CORES * OWN
    slots = chips * OWN
    positions = prompt_keys.shape[0]
    blocks = key_scale.shape[0]
    limit = suffix_key_rows.shape[1]
    depth, columns = out_weight.shape
    out_rows = samples // groups
    any_spec = pl.BlockSpec(memory_space=pl.ANY)
    return pl.pallas_call(
        functools.partial(kernel, chips, groups),
        out_shape=pltpu.VMEM((out_rows, columns), F32),
        in_specs=[any_spec] * 10,
        out_specs=pl.BlockSpec(memory_space=pltpu.VMEM),
        scratch_shapes=[
            pltpu.VMEM(queries.shape, BF16),
            pltpu.VMEM((1, samples), jnp.int32),
            pltpu.SMEM((OWN,), jnp.int32),
            pltpu.VMEM((CORES, positions, WIDTH), BF16),
            pltpu.VMEM((CORES, positions, WIDTH), BF16),
            pltpu.VMEM((1, blocks), F32),
            pltpu.VMEM((1, blocks), F32),
            pltpu.VMEM((CORES, 2 * blocks, WIDTH), F32),
            pltpu.VMEM((OWN, limit, WIDTH), BF16),
            pltpu.VMEM((OWN, limit, WIDTH), BF16),
            pltpu.VMEM((CORES, columns, depth), BF16),
            pltpu.VMEM((ROWS, WIDTH), F32),
            pltpu.VMEM((CORES, chips, ROWS, WIDTH), BF16),
            pltpu.VMEM((samples * GROUP, WIDTH), F32),
            pltpu.VMEM((slots * GROUP, WIDTH), F32),
            pltpu.VMEM((slots * GROUP, WIDTH), BF16),
            pltpu.VMEM((chips, 1, WIDTH), F32),
            pltpu.VMEM((chips, ROWS, WIDTH), BF16),
            pltpu.VMEM((chips, 1, WIDTH), F32),
            pltpu.VMEM((chips, ROWS, WIDTH), BF16),
            pltpu.VMEM((groups, slots // groups * GROUP, WIDTH), F32),
            pltpu.VMEM((CORES, groups, slots // groups, columns), F32),
            pltpu.VMEM((CORES * groups, slots // groups, columns), F32),
            pltpu.SemaphoreType.DMA((10,)),
            pltpu.SemaphoreType.DMA((10,)),
            pltpu.SemaphoreType.DMA((10,)),
            pltpu.SemaphoreType.DMA((chips // ROW_CHIPS,)),
        ],
        compiler_params=pltpu.CompilerParams(
            collective_id=0, has_side_effects=True, vmem_limit_bytes=60 * 1024 * 1024
        ),
        name="decode_attention",
    )(
        queries,
        owner_slot.reshape(1, samples),
        suffix_len,
        prompt_keys,
        prompt_value_rows,
        key_scale.reshape(1, blocks),
        value_block_scale.reshape(1, blocks),
        suffix_key_rows,
        suffix_value_rows,
        out_weight.T,
    )


def solution(mesh):
    in_specs = (
        P("seq", "kv"),
        P(),
        P("seq"),
        P("seq", "kv"),
        P("seq", "kv"),
        P("seq", "kv"),
        P("seq", "kv"),
        P("seq", None, "kv"),
        P("seq", None, "kv"),
        P("kv", "seq"),
    )
    out_specs = P("kv", "seq")
    return jax.shard_map(local, mesh=mesh, in_specs=in_specs, out_specs=out_specs, check_vma=False)
```

```python
import functools

import jax
import jax.numpy as jnp
from jax import lax
from jax.experimental import pallas as pl
from jax.experimental.pallas import tpu as pltpu
from jax.sharding import PartitionSpec as P

MESH = pl.DeviceIdType.MESH
F32 = jnp.float32
BF16 = jnp.bfloat16
LOG2E = 1.4426950408889634
NEG_FILL = -1e30

CORES = 2
ROW_CHIPS = 4
GROUP = 8
WIDTH = 128
OWN = 2
ROWS = OWN * GROUP
SPAN = 128

SQ, SC, SK, SV, SW, SF, SN, SS, SA, SY = range(10)
LQ, LO, LK, LV, LKS, LVS, LW, LSK, LSV, LSL = range(10)


def nt_dot(a, b):
    return lax.dot_general(a, b, (((1,), (1,)), ((), ())), preferred_element_type=F32)


def near_pairs(size):
    pairs = [[0]] + [[step, size - step] for step in range(1, size // 2)] + [[size // 2]]
    places = iter(range(size))
    return [[(next(places), k) for k in pair] for pair in pairs]


def kernel(
    chips,
    groups,
    q_hbm,
    os_hbm,
    sl_hbm,
    k_hbm,
    v_hbm,
    ks_hbm,
    vs_hbm,
    sk_hbm,
    sv_hbm,
    w_hbm,
    o_ref,
    qown,
    osv,
    sls,
    kbuf,
    vbuf,
    ksv,
    vsv,
    scb,
    skb,
    svb,
    wbuf,
    q32,
    qg,
    qf32,
    qs32,
    nsend,
    ssend,
    nrecv,
    srecv,
    att,
    a32,
    ysend,
    yrecv,
    ssem,
    rsem,
    lsem,
    asem,
):
    me = lax.axis_index("seq")
    y = lax.axis_index("kv")
    c = lax.rem(me, CORES)
    chip = me // CORES
    other = 1 - c
    depth_chips = chips // ROW_CHIPS

    def load(src, dst, i):
        cp = pltpu.make_async_copy(src, dst, lsem.at[i])
        cp.start()
        return cp

    def remote(src, dst, i, seq, kv):
        return pltpu.make_async_remote_copy(
            src_ref=src,
            dst_ref=dst,
            send_sem=ssem.at[i],
            recv_sem=rsem.at[i],
            device_id={"kv": kv, "seq": seq},
            device_id_type=MESH,
        )

    load_q = load(q_hbm, qown, LQ)

    def far_first(k):
        a, b = k // ROW_CHIPS, lax.rem(k, ROW_CHIPS)
        return lax.rem(chip // ROW_CHIPS + far_offset(a, depth_chips), depth_chips) * ROW_CHIPS + far_in_row(b)

    def far_in_row(b):
        return lax.rem(chip + far_offset(b, ROW_CHIPS), ROW_CHIPS)

    def far_offset(k, size):
        step = jnp.where(lax.rem(k, 2) == 0, size // 2 - k // 2, size // 2 + (k + 1) // 2)
        return jnp.where(k == size - 1, 0, step)

    barrier = pltpu.get_barrier_semaphore()

    def greet(seq, kv):
        pl.semaphore_signal(barrier, inc=1, device_id={"kv": kv, "seq": seq}, device_id_type=MESH)

    def greet_plane(k, carry):
        greet(far_first(k) * CORES + c, y)
        return carry

    lax.fori_loop(0, chips - 1, greet_plane, 0, unroll=True)

    def greet_column(k, carry):
        kv = lax.rem(y + far_offset(k, groups), groups)
        greet(chip * CORES + c, kv)
        greet(chip * CORES + other, kv)
        return carry

    lax.fori_loop(0, groups - 1, greet_column, 0, unroll=True)
    greet(chip * CORES + other, y)

    load_o = load(os_hbm, osv, LO)
    load_ks = load(ks_hbm, ksv, LKS)
    load_vs = load(vs_hbm, vsv, LVS)
    load_k = load(k_hbm, kbuf.at[c], LK)
    load_v = load(v_hbm, vbuf.at[c], LV)
    load_w = load(w_hbm, wbuf.at[c], LW)
    load_sk = load(sk_hbm, skb, LSK)
    load_sv = load(sv_hbm, svb, LSV)
    load_sl = load(sl_hbm, sls, LSL)

    load_q.wait()
    for h in range(GROUP):
        piece = qown[:, h * WIDTH : (h + 1) * WIDTH].astype(F32)
        for s in range(OWN):
            q32[s * GROUP + h : s * GROUP + h + 1, :] = piece[s : s + 1, :]
    qg[c, chip] = q32[...].astype(BF16)

    pl.semaphore_wait(barrier, (chips - 1) + 2 * (groups - 1) + 1)

    def send_queries(k, carry):
        remote(qg.at[c, chip], qg.at[c, chip], SQ, far_first(k) * CORES + c, y).start()
        return carry

    lax.fori_loop(0, chips - 1, send_queries, 0, unroll=True)

    partner = chip * CORES + other
    swap_k = remote(k_hbm, kbuf.at[c], SK, partner, y)
    swap_k.start()
    swap_v = remote(v_hbm, vbuf.at[c], SV, partner, y)
    swap_v.start()
    swap_w = remote(w_hbm, wbuf.at[c], SW, partner, y)
    swap_w.start()
    load_ks.wait()
    load_vs.wait()
    blocks = ksv.shape[1]
    scb[c, 0:blocks, :] = jnp.concatenate(
        [jnp.broadcast_to(ksv[:, b : b + 1] * (WIDTH**-0.5 * LOG2E), (1, WIDTH)) for b in range(blocks)], axis=0
    )
    scb[c, blocks : 2 * blocks, :] = jnp.concatenate(
        [jnp.broadcast_to(vsv[:, b : b + 1], (1, WIDTH)) for b in range(blocks)], axis=0
    )
    swap_f = remote(scb.at[c], scb.at[c], SF, partner, y)
    swap_f.start()

    load_o.wait()
    samples = chips * CORES * OWN
    slots = chips * OWN
    s_i = lax.broadcasted_iota(jnp.int32, (samples, samples), 0)
    m_i = lax.broadcasted_iota(jnp.int32, (samples, samples), 1)
    m_in = lax.rem(m_i, slots)
    s_of_m = (m_in // OWN) * (CORES * OWN) + (m_i // slots) * OWN + lax.rem(m_i, OWN)
    spread = jnp.where(s_i == s_of_m, 1.0, 0.0).astype(BF16)
    owner_rows = jnp.broadcast_to(osv[...].astype(F32), (16, samples)).astype(BF16)
    owner = jnp.dot(owner_rows, spread, preferred_element_type=F32)[0:1, :]
    i_i = lax.broadcasted_iota(jnp.int32, (slots, samples), 0)
    slot_i = (i_i // OWN) * (CORES * OWN) + c * OWN + lax.rem(i_i, OWN)
    pick = jnp.where(owner == slot_i.astype(F32), 1.0, 0.0).astype(BF16)

    many_q = qg.at[0, pl.ds(0, chips - 1)]
    remote(many_q, many_q, SQ, partner, y).wait_recv()
    swap_q = remote(qg.at[c], qg.at[c], SC, partner, y)
    swap_q.start()
    swap_q.wait_recv()

    qf32[...] = qg[...].reshape(samples * GROUP, WIDTH).astype(F32)
    by_head = jnp.concatenate(
        [qf32[pl.ds(h, samples, stride=GROUP), :].astype(BF16) for h in range(GROUP)], axis=1
    )
    picked = jnp.dot(pick, by_head, preferred_element_type=F32)
    for h in range(GROUP):
        qs32[pl.ds(h, slots, stride=GROUP), :] = picked[:, h * WIDTH : (h + 1) * WIDTH]

    load_k.wait()
    load_v.wait()
    swap_k.wait_recv()
    swap_v.wait_recv()
    swap_f.wait_recv()

    chunk_chips = 8
    chunk = chunk_chips * ROWS
    chunks = chips // chunk_chips
    row_in = lax.rem(lax.broadcasted_iota(jnp.int32, (chunk, WIDTH), 0), ROWS)
    lane = lax.broadcasted_iota(jnp.int32, (chunk, WIDTH), 1)

    def prompt_chunk(n):
        first = pl.multiple_of(n * chunk, chunk)
        qc = qs32[pl.ds(first, chunk), :].astype(BF16)
        parts = []
        for core in range(CORES):
            s = nt_dot(qc, kbuf[core])
            for b in range(blocks):
                parts.append(s[:, b * SPAN : (b + 1) * SPAN] * scb[core, b : b + 1, :])
        peak = functools.reduce(jnp.maximum, parts)
        peak = jnp.max(peak, axis=1, keepdims=True)
        parts = [jnp.exp2(s - peak) for s in parts]
        total = jnp.sum(functools.reduce(jnp.add, parts), axis=1, keepdims=True)
        numer = None
        for core in range(CORES):
            scaled = jnp.concatenate(
                [
                    (parts[core * blocks + b] * scb[core, blocks + b : blocks + b + 1, :]).astype(BF16)
                    for b in range(blocks)
                ],
                axis=1,
            )
            term = jnp.dot(scaled, vbuf[core], preferred_element_type=F32)
            numer = term if numer is None else numer + term
        nsend[pl.ds(first, chunk), :] = numer.astype(BF16)
        stats = jnp.where(lane == row_in, peak, 0.0) + jnp.where(lane == row_in + ROWS, total, 0.0)
        stats = jnp.sum(stats.reshape(chunk_chips, ROWS, WIDTH), axis=1)
        for i in range(chunk_chips):
            ssend[n * chunk_chips + i] = stats[i : i + 1, :]

    def send_partial(t):
        first = pl.multiple_of(t * ROWS, ROWS)
        remote(ssend.at[t], srecv.at[chip], SS, t * CORES + c, y).start()
        remote(nsend.at[pl.ds(first, ROWS)], nrecv.at[chip], SN, t * CORES + c, y).start()

    own_chunk = chip // chunk_chips

    def chunk_step(k, carry):
        off = lax.rem(k + chunks // 2, chunks)
        n = lax.rem(own_chunk + off, chunks)
        prompt_chunk(n)

        def send_one(i, inner):
            t = n * chunk_chips + (i // ROW_CHIPS) * ROW_CHIPS + far_in_row(lax.rem(i, ROW_CHIPS))

            @pl.when(t != chip)
            def _():
                send_partial(t)

            return inner

        lax.fori_loop(0, chunk_chips, send_one, 0, unroll=True)
        return carry

    lax.fori_loop(0, chunks, chunk_step, 0)
    own_first = pl.multiple_of(chip * ROWS, ROWS)
    nrecv[chip] = nsend[pl.ds(own_first, ROWS), :]
    srecv[chip] = ssend[chip]

    load_sk.wait()
    load_sv.wait()
    load_sl.wait()
    own_q = qs32[pl.ds(own_first, ROWS), :].astype(BF16)
    limit = skb.shape[1]
    live_i = lax.broadcasted_iota(jnp.int32, (GROUP, limit), 1)
    near_numer, near_peak, near_total = [], [], []
    for j in range(OWN):
        live = live_i < sls[j]
        s = nt_dot(own_q, skb[j])[j * GROUP : (j + 1) * GROUP, :] * (WIDTH**-0.5 * LOG2E)
        s = jnp.where(live, s, NEG_FILL)
        peak = jnp.max(s, axis=1, keepdims=True)
        w = jnp.where(live, jnp.exp2(s - peak), 0.0)
        near_total.append(jnp.sum(w, axis=1, keepdims=True))
        near_peak.append(peak)
        w16 = jnp.concatenate([w, jnp.zeros_like(w)], axis=0).astype(BF16)
        near_numer.append(jnp.dot(w16, svb[j], preferred_element_type=F32)[:GROUP])
    near_numer = jnp.concatenate(near_numer, axis=0)
    near_peak = jnp.concatenate(near_peak, axis=0)
    near_total = jnp.concatenate(near_total, axis=0)

    many_s = srecv.at[pl.ds(0, chips - 1)]
    remote(many_s, many_s, SS, partner, y).wait_recv()
    stats = jnp.concatenate([srecv[i] for i in range(chips)], axis=0)
    stats = jnp.concatenate([stats, jnp.zeros((WIDTH - chips, WIDTH), F32)], axis=0)
    stats = jnp.transpose(stats)
    peaks = stats[0:ROWS, 0:chips]
    totals = stats[ROWS : 2 * ROWS, 0:chips]
    peak = jnp.maximum(jnp.max(peaks, axis=1, keepdims=True), near_peak)
    factor = jnp.exp2(peaks - peak)
    near_factor = jnp.exp2(near_peak - peak)
    total = jnp.sum(factor * totals, axis=1, keepdims=True) + near_total * near_factor
    many_n = nrecv.at[pl.ds(0, chips - 1)]
    remote(many_n, many_n, SN, partner, y).wait_recv()
    numer = near_numer * near_factor
    for i in range(chips):
        numer = numer + nrecv[i].astype(F32) * factor[:, i : i + 1]
    att[chip] = (numer / total).astype(BF16)

    row = chip // ROW_CHIPS

    def send_att(to, t):
        pltpu.make_async_remote_copy(
            src_ref=att.at[chip],
            dst_ref=att.at[chip],
            send_sem=ssem.at[SA],
            recv_sem=asem.at[lax.rem(to - row + depth_chips, depth_chips)],
            device_id={"kv": y, "seq": t * CORES + c},
            device_id_type=MESH,
        ).start()

    for to in range(depth_chips):
        for b in range(ROW_CHIPS):
            t = to * ROW_CHIPS + far_in_row(b)
            if b < ROW_CHIPS - 1:
                send_att(to, t)
            else:
                pl.when(t != chip)(functools.partial(send_att, to, t))
    load_w.wait()
    swap_w.wait_recv()
    per_group = ROW_CHIPS * OWN
    for pair in near_pairs(depth_chips):
        ts = [lax.rem(row + depth_chips - k, depth_chips) for _, k in pair]
        for (n, k), t in zip(pair, ts):
            arrived = att.at[pl.ds(0, ROW_CHIPS - (k == 0))]
            pltpu.make_async_remote_copy(
                src_ref=arrived,
                dst_ref=arrived,
                send_sem=ssem.at[SA],
                recv_sem=asem.at[k],
                device_id={"kv": y, "seq": partner},
                device_id_type=MESH,
            ).wait_recv()
            first = pl.multiple_of(t * ROW_CHIPS, ROW_CHIPS)
            a32[n] = att[pl.ds(first, ROW_CHIPS)].reshape(per_group * GROUP, WIDTH).astype(F32)
        rows = jnp.concatenate(
            [
                jnp.concatenate([a32[n, pl.ds(h, per_group, stride=GROUP), :] for n, _ in pair], axis=0).astype(BF16)
                for h in range(GROUP)
            ],
            axis=1,
        )
        for core in range(CORES):
            part = nt_dot(rows, wbuf[core])
            for m, (n, _) in enumerate(pair):
                ysend[core, n] = part[m * per_group : (m + 1) * per_group, :]
        for (n, _), t in zip(pair, ts):
            remote(ysend.at[other, n], yrecv.at[c * groups + y], SY, chip * CORES + other, t).start()

            @pl.when(t != y)
            def _():
                remote(ysend.at[c, n], yrecv.at[c * groups + y], SY, chip * CORES + c, t).start()

            @pl.when(t == y)
            def _():
                yrecv[c * groups + y] = ysend[c, n]

    many_y = yrecv.at[pl.ds(0, CORES * groups - 1)]
    last = remote(many_y, many_y, SY, partner, y)
    last.wait_recv()
    for core in range(CORES):
        acc = yrecv[core * groups]
        for i in range(1, groups):
            acc = acc + yrecv[core * groups + i]
        for q in range(per_group // OWN):
            first = q * CORES * OWN + core * OWN
            o_ref[first : first + OWN, :] = acc[q * OWN : (q + 1) * OWN, :]

    remote(many_q, many_q, SQ, partner, y).wait_send()
    swap_q.wait_send()
    swap_k.wait_send()
    swap_v.wait_send()
    swap_w.wait_send()
    swap_f.wait_send()
    remote(many_s, many_s, SS, partner, y).wait_send()
    remote(many_n, many_n, SN, partner, y).wait_send()
    many_a = att.at[pl.ds(0, chips - 1)]
    remote(many_a, many_a, SA, partner, y).wait_send()
    last.wait_send()


def local(
    queries,
    owner_slot,
    suffix_len,
    prompt_keys,
    prompt_value_rows,
    key_scale,
    value_block_scale,
    suffix_key_rows,
    suffix_value_rows,
    out_weight,
):
    groups = lax.axis_size("kv")
    chips = lax.axis_size("seq") // CORES
    samples = chips * CORES * OWN
    slots = chips * OWN
    positions = prompt_keys.shape[0]
    blocks = key_scale.shape[0]
    limit = suffix_key_rows.shape[1]
    depth, columns = out_weight.shape
    out_rows = samples // groups
    any_spec = pl.BlockSpec(memory_space=pl.ANY)
    return pl.pallas_call(
        functools.partial(kernel, chips, groups),
        out_shape=pltpu.VMEM((out_rows, columns), F32),
        in_specs=[any_spec] * 10,
        out_specs=pl.BlockSpec(memory_space=pltpu.VMEM),
        scratch_shapes=[
            pltpu.VMEM(queries.shape, BF16),
            pltpu.VMEM((1, samples), jnp.int32),
            pltpu.SMEM((OWN,), jnp.int32),
            pltpu.VMEM((CORES, positions, WIDTH), BF16),
            pltpu.VMEM((CORES, positions, WIDTH), BF16),
            pltpu.VMEM((1, blocks), F32),
            pltpu.VMEM((1, blocks), F32),
            pltpu.VMEM((CORES, 2 * blocks, WIDTH), F32),
            pltpu.VMEM((OWN, limit, WIDTH), BF16),
            pltpu.VMEM((OWN, limit, WIDTH), BF16),
            pltpu.VMEM((CORES, columns, depth), BF16),
            pltpu.VMEM((ROWS, WIDTH), F32),
            pltpu.VMEM((CORES, chips, ROWS, WIDTH), BF16),
            pltpu.VMEM((samples * GROUP, WIDTH), F32),
            pltpu.VMEM((slots * GROUP, WIDTH), F32),
            pltpu.VMEM((slots * GROUP, WIDTH), BF16),
            pltpu.VMEM((chips, 1, WIDTH), F32),
            pltpu.VMEM((chips, ROWS, WIDTH), BF16),
            pltpu.VMEM((chips, 1, WIDTH), F32),
            pltpu.VMEM((chips, ROWS, WIDTH), BF16),
            pltpu.VMEM((groups, slots // groups * GROUP, WIDTH), F32),
            pltpu.VMEM((CORES, groups, slots // groups, columns), F32),
            pltpu.VMEM((CORES * groups, slots // groups, columns), F32),
            pltpu.SemaphoreType.DMA((10,)),
            pltpu.SemaphoreType.DMA((10,)),
            pltpu.SemaphoreType.DMA((10,)),
            pltpu.SemaphoreType.DMA((chips // ROW_CHIPS,)),
        ],
        compiler_params=pltpu.CompilerParams(
            collective_id=0, has_side_effects=True, vmem_limit_bytes=60 * 1024 * 1024
        ),
        name="decode_attention",
    )(
        queries,
        owner_slot.reshape(1, samples),
        suffix_len,
        prompt_keys,
        prompt_value_rows,
        key_scale.reshape(1, blocks),
        value_block_scale.reshape(1, blocks),
        suffix_key_rows,
        suffix_value_rows,
        out_weight.T,
    )


def solution(mesh):
    in_specs = (
        P("seq", "kv"),
        P(),
        P("seq"),
        P("seq", "kv"),
        P("seq", "kv"),
        P("seq", "kv"),
        P("seq", "kv"),
        P("seq", None, "kv"),
        P("seq", None, "kv"),
        P("kv", "seq"),
    )
    out_specs = P("kv", "seq")
    return jax.shard_map(local, mesh=mesh, in_specs=in_specs, out_specs=out_specs, check_vma=False)
```

```python
import functools

import jax
import jax.numpy as jnp
from jax import lax
from jax.experimental import pallas as pl
from jax.experimental.pallas import tpu as pltpu
from jax.sharding import PartitionSpec as P

MESH = pl.DeviceIdType.MESH
F32 = jnp.float32
BF16 = jnp.bfloat16
LOG2E = 1.4426950408889634
NEG_FILL = -1e30

CORES = 2
ROW_CHIPS = 4
GROUP = 8
WIDTH = 128
OWN = 2
ROWS = OWN * GROUP
SPAN = 128

SQ, SC, SK, SV, SW, SF, SN, SS, SA, SY = range(10)
LQ, LO, LK, LV, LKS, LVS, LW, LSK, LSV, LSL = range(10)


def nt_dot(a, b):
    return lax.dot_general(a, b, (((1,), (1,)), ((), ())), preferred_element_type=F32)


def near_pairs(size):
    pairs = [[0]] + [[step, size - step] for step in range(1, size // 2)] + [[size // 2]]
    places = iter(range(size))
    return [[(next(places), k) for k in pair] for pair in pairs]


def kernel(
    chips,
    groups,
    q_hbm,
    os_hbm,
    sl_hbm,
    k_hbm,
    v_hbm,
    ks_hbm,
    vs_hbm,
    sk_hbm,
    sv_hbm,
    w_hbm,
    o_ref,
    qown,
    osv,
    sls,
    kbuf,
    vbuf,
    ksv,
    vsv,
    scb,
    skb,
    svb,
    wbuf,
    q32,
    qg,
    qf32,
    qs32,
    nsend,
    ssend,
    nrecv,
    srecv,
    att,
    a32,
    ysend,
    yrecv,
    ssem,
    rsem,
    lsem,
    asem,
):
    me = lax.axis_index("seq")
    y = lax.axis_index("kv")
    c = lax.rem(me, CORES)
    chip = me // CORES
    other = 1 - c
    depth_chips = chips // ROW_CHIPS

    def load(src, dst, i):
        cp = pltpu.make_async_copy(src, dst, lsem.at[i])
        cp.start()
        return cp

    def remote(src, dst, i, seq, kv):
        return pltpu.make_async_remote_copy(
            src_ref=src,
            dst_ref=dst,
            send_sem=ssem.at[i],
            recv_sem=rsem.at[i],
            device_id={"kv": kv, "seq": seq},
            device_id_type=MESH,
        )

    load_q = load(q_hbm, qown, LQ)

    def far_first(k):
        a, b = k // ROW_CHIPS, lax.rem(k, ROW_CHIPS)
        return lax.rem(chip // ROW_CHIPS + far_offset(a, depth_chips), depth_chips) * ROW_CHIPS + far_in_row(b)

    def far_in_row(b):
        return lax.rem(chip + far_offset(b, ROW_CHIPS), ROW_CHIPS)

    def far_offset(k, size):
        step = jnp.where(lax.rem(k, 2) == 0, size // 2 - k // 2, size // 2 + (k + 1) // 2)
        return jnp.where(k == size - 1, 0, step)

    barrier = pltpu.get_barrier_semaphore()

    def greet(seq, kv):
        pl.semaphore_signal(barrier, inc=1, device_id={"kv": kv, "seq": seq}, device_id_type=MESH)

    def greet_plane(k, carry):
        greet(far_first(k) * CORES + c, y)
        return carry

    lax.fori_loop(0, chips - 1, greet_plane, 0, unroll=True)

    def greet_column(k, carry):
        kv = lax.rem(y + far_offset(k, groups), groups)
        greet(chip * CORES + c, kv)
        greet(chip * CORES + other, kv)
        return carry

    lax.fori_loop(0, groups - 1, greet_column, 0, unroll=True)
    greet(chip * CORES + other, y)

    load_o = load(os_hbm, osv, LO)
    load_ks = load(ks_hbm, ksv, LKS)
    load_vs = load(vs_hbm, vsv, LVS)
    load_k = load(k_hbm, kbuf.at[c], LK)
    load_v = load(v_hbm, vbuf.at[c], LV)
    load_w = load(w_hbm, wbuf.at[c], LW)
    load_sk = load(sk_hbm, skb, LSK)
    load_sv = load(sv_hbm, svb, LSV)
    load_sl = load(sl_hbm, sls, LSL)

    load_q.wait()
    for h in range(GROUP):
        piece = qown[:, h * WIDTH : (h + 1) * WIDTH].astype(F32)
        for s in range(OWN):
            q32[s * GROUP + h : s * GROUP + h + 1, :] = piece[s : s + 1, :]
    qg[c, chip] = q32[...].astype(BF16)

    pl.semaphore_wait(barrier, (chips - 1) + 2 * (groups - 1) + 1)

    def send_queries(k, carry):
        remote(qg.at[c, chip], qg.at[c, chip], SQ, far_first(k) * CORES + c, y).start()
        return carry

    lax.fori_loop(0, chips - 1, send_queries, 0, unroll=True)

    partner = chip * CORES + other
    swap_k = remote(k_hbm, kbuf.at[c], SK, partner, y)
    swap_k.start()
    swap_v = remote(v_hbm, vbuf.at[c], SV, partner, y)
    swap_v.start()
    swap_w = remote(w_hbm, wbuf.at[c], SW, partner, y)
    swap_w.start()
    load_ks.wait()
    load_vs.wait()
    blocks = ksv.shape[1]
    scb[c, 0:blocks, :] = jnp.concatenate(
        [jnp.broadcast_to(ksv[:, b : b + 1] * (WIDTH**-0.5 * LOG2E), (1, WIDTH)) for b in range(blocks)], axis=0
    )
    scb[c, blocks : 2 * blocks, :] = jnp.concatenate(
        [jnp.broadcast_to(vsv[:, b : b + 1], (1, WIDTH)) for b in range(blocks)], axis=0
    )
    swap_f = remote(scb.at[c], scb.at[c], SF, partner, y)
    swap_f.start()

    load_o.wait()
    samples = chips * CORES * OWN
    slots = chips * OWN
    s_i = lax.broadcasted_iota(jnp.int32, (samples, samples), 0)
    m_i = lax.broadcasted_iota(jnp.int32, (samples, samples), 1)
    m_in = lax.rem(m_i, slots)
    s_of_m = (m_in // OWN) * (CORES * OWN) + (m_i // slots) * OWN + lax.rem(m_i, OWN)
    spread = jnp.where(s_i == s_of_m, 1.0, 0.0).astype(BF16)
    owner_rows = jnp.broadcast_to(osv[...].astype(F32), (16, samples)).astype(BF16)
    owner = jnp.dot(owner_rows, spread, preferred_element_type=F32)[0:1, :]
    i_i = lax.broadcasted_iota(jnp.int32, (slots, samples), 0)
    slot_i = (i_i // OWN) * (CORES * OWN) + c * OWN + lax.rem(i_i, OWN)
    pick = jnp.where(owner == slot_i.astype(F32), 1.0, 0.0).astype(BF16)

    many_q = qg.at[0, pl.ds(0, chips - 1)]
    remote(many_q, many_q, SQ, partner, y).wait_recv()
    swap_q = remote(qg.at[c], qg.at[c], SC, partner, y)
    swap_q.start()
    swap_q.wait_recv()

    qf32[...] = qg[...].reshape(samples * GROUP, WIDTH).astype(F32)
    by_head = jnp.concatenate(
        [qf32[pl.ds(h, samples, stride=GROUP), :].astype(BF16) for h in range(GROUP)], axis=1
    )
    picked = jnp.dot(pick, by_head, preferred_element_type=F32)
    for h in range(GROUP):
        qs32[pl.ds(h, slots, stride=GROUP), :] = picked[:, h * WIDTH : (h + 1) * WIDTH]

    load_k.wait()
    load_v.wait()
    swap_k.wait_recv()
    swap_v.wait_recv()
    swap_f.wait_recv()

    chunk_chips = ROW_CHIPS
    chunk = chunk_chips * ROWS
    chunks = chips // chunk_chips
    row_in = lax.rem(lax.broadcasted_iota(jnp.int32, (chunk, WIDTH), 0), ROWS)
    lane = lax.broadcasted_iota(jnp.int32, (chunk, WIDTH), 1)

    def prompt_chunk(n):
        first = pl.multiple_of(n * chunk, chunk)
        qc = qs32[pl.ds(first, chunk), :].astype(BF16)
        parts = []
        for core in range(CORES):
            s = nt_dot(qc, kbuf[core])
            for b in range(blocks):
                parts.append(s[:, b * SPAN : (b + 1) * SPAN] * scb[core, b : b + 1, :])
        peak = functools.reduce(jnp.maximum, parts)
        peak = jnp.max(peak, axis=1, keepdims=True)
        parts = [jnp.exp2(s - peak) for s in parts]
        total = jnp.sum(functools.reduce(jnp.add, parts), axis=1, keepdims=True)
        numer = None
        for core in range(CORES):
            scaled = jnp.concatenate(
                [
                    (parts[core * blocks + b] * scb[core, blocks + b : blocks + b + 1, :]).astype(BF16)
                    for b in range(blocks)
                ],
                axis=1,
            )
            term = jnp.dot(scaled, vbuf[core], preferred_element_type=F32)
            numer = term if numer is None else numer + term
        nsend[pl.ds(first, chunk), :] = numer.astype(BF16)
        stats = jnp.where(lane == row_in, peak, 0.0) + jnp.where(lane == row_in + ROWS, total, 0.0)
        stats = jnp.sum(stats.reshape(chunk_chips, ROWS, WIDTH), axis=1)
        for i in range(chunk_chips):
            ssend[n * chunk_chips + i] = stats[i : i + 1, :]

    def send_partial(t):
        first = pl.multiple_of(t * ROWS, ROWS)
        remote(ssend.at[t], srecv.at[chip], SS, t * CORES + c, y).start()
        remote(nsend.at[pl.ds(first, ROWS)], nrecv.at[chip], SN, t * CORES + c, y).start()

    own_chunk = chip // chunk_chips

    def chunk_step(k, carry):
        n = lax.rem(own_chunk + far_offset(k, chunks), chunks)
        prompt_chunk(n)

        def send_one(i, inner):
            t = n * chunk_chips + far_in_row(i)

            @pl.when(t != chip)
            def _():
                send_partial(t)

            return inner

        lax.fori_loop(0, chunk_chips, send_one, 0, unroll=True)
        return carry

    lax.fori_loop(0, chunks, chunk_step, 0)
    own_first = pl.multiple_of(chip * ROWS, ROWS)
    nrecv[chip] = nsend[pl.ds(own_first, ROWS), :]
    srecv[chip] = ssend[chip]

    load_sk.wait()
    load_sv.wait()
    load_sl.wait()
    own_q = qs32[pl.ds(own_first, ROWS), :].astype(BF16)
    limit = skb.shape[1]
    live_i = lax.broadcasted_iota(jnp.int32, (GROUP, limit), 1)
    near_numer, near_peak, near_total = [], [], []
    for j in range(OWN):
        live = live_i < sls[j]
        s = nt_dot(own_q, skb[j])[j * GROUP : (j + 1) * GROUP, :] * (WIDTH**-0.5 * LOG2E)
        s = jnp.where(live, s, NEG_FILL)
        peak = jnp.max(s, axis=1, keepdims=True)
        w = jnp.where(live, jnp.exp2(s - peak), 0.0)
        near_total.append(jnp.sum(w, axis=1, keepdims=True))
        near_peak.append(peak)
        w16 = jnp.concatenate([w, jnp.zeros_like(w)], axis=0).astype(BF16)
        near_numer.append(jnp.dot(w16, svb[j], preferred_element_type=F32)[:GROUP])
    near_numer = jnp.concatenate(near_numer, axis=0)
    near_peak = jnp.concatenate(near_peak, axis=0)
    near_total = jnp.concatenate(near_total, axis=0)

    many_s = srecv.at[pl.ds(0, chips - 1)]
    remote(many_s, many_s, SS, partner, y).wait_recv()
    stats = jnp.concatenate([srecv[i] for i in range(chips)], axis=0)
    stats = jnp.concatenate([stats, jnp.zeros((WIDTH - chips, WIDTH), F32)], axis=0)
    stats = jnp.transpose(stats)
    peaks = stats[0:ROWS, 0:chips]
    totals = stats[ROWS : 2 * ROWS, 0:chips]
    peak = jnp.maximum(jnp.max(peaks, axis=1, keepdims=True), near_peak)
    factor = jnp.exp2(peaks - peak)
    near_factor = jnp.exp2(near_peak - peak)
    total = jnp.sum(factor * totals, axis=1, keepdims=True) + near_total * near_factor
    many_n = nrecv.at[pl.ds(0, chips - 1)]
    remote(many_n, many_n, SN, partner, y).wait_recv()
    numer = near_numer * near_factor
    for i in range(chips):
        numer = numer + nrecv[i].astype(F32) * factor[:, i : i + 1]
    att[chip] = (numer / total).astype(BF16)

    row = chip // ROW_CHIPS

    def send_att(to, t):
        pltpu.make_async_remote_copy(
            src_ref=att.at[chip],
            dst_ref=att.at[chip],
            send_sem=ssem.at[SA],
            recv_sem=asem.at[lax.rem(to - row + depth_chips, depth_chips)],
            device_id={"kv": y, "seq": t * CORES + c},
            device_id_type=MESH,
        ).start()

    for to in range(depth_chips):
        for b in range(ROW_CHIPS):
            t = to * ROW_CHIPS + b
            pl.when(t != chip)(functools.partial(send_att, to, t))
    load_w.wait()
    swap_w.wait_recv()
    per_group = ROW_CHIPS * OWN
    for pair in near_pairs(depth_chips):
        ts = [lax.rem(row + depth_chips - k, depth_chips) for _, k in pair]
        for (n, k), t in zip(pair, ts):
            arrived = att.at[pl.ds(0, ROW_CHIPS - (k == 0))]
            pltpu.make_async_remote_copy(
                src_ref=arrived,
                dst_ref=arrived,
                send_sem=ssem.at[SA],
                recv_sem=asem.at[k],
                device_id={"kv": y, "seq": partner},
                device_id_type=MESH,
            ).wait_recv()
            first = pl.multiple_of(t * ROW_CHIPS, ROW_CHIPS)
            a32[n] = att[pl.ds(first, ROW_CHIPS)].reshape(per_group * GROUP, WIDTH).astype(F32)
        rows = jnp.concatenate(
            [
                jnp.concatenate([a32[n, pl.ds(h, per_group, stride=GROUP), :] for n, _ in pair], axis=0).astype(BF16)
                for h in range(GROUP)
            ],
            axis=1,
        )
        for core in range(CORES):
            part = nt_dot(rows, wbuf[core])
            for m, (n, _) in enumerate(pair):
                ysend[core, n] = part[m * per_group : (m + 1) * per_group, :]
        for (n, _), t in zip(pair, ts):
            remote(ysend.at[other, n], yrecv.at[c * groups + y], SY, chip * CORES + other, t).start()

            @pl.when(t != y)
            def _():
                remote(ysend.at[c, n], yrecv.at[c * groups + y], SY, chip * CORES + c, t).start()

            @pl.when(t == y)
            def _():
                yrecv[c * groups + y] = ysend[c, n]

    many_y = yrecv.at[pl.ds(0, CORES * groups - 1)]
    last = remote(many_y, many_y, SY, partner, y)
    last.wait_recv()
    for core in range(CORES):
        acc = yrecv[core * groups]
        for i in range(1, groups):
            acc = acc + yrecv[core * groups + i]
        for q in range(per_group // OWN):
            first = q * CORES * OWN + core * OWN
            o_ref[first : first + OWN, :] = acc[q * OWN : (q + 1) * OWN, :]

    remote(many_q, many_q, SQ, partner, y).wait_send()
    swap_q.wait_send()
    swap_k.wait_send()
    swap_v.wait_send()
    swap_w.wait_send()
    swap_f.wait_send()
    remote(many_s, many_s, SS, partner, y).wait_send()
    remote(many_n, many_n, SN, partner, y).wait_send()
    many_a = att.at[pl.ds(0, chips - 1)]
    remote(many_a, many_a, SA, partner, y).wait_send()
    last.wait_send()


def local(
    queries,
    owner_slot,
    suffix_len,
    prompt_keys,
    prompt_value_rows,
    key_scale,
    value_block_scale,
    suffix_key_rows,
    suffix_value_rows,
    out_weight,
):
    groups = lax.axis_size("kv")
    chips = lax.axis_size("seq") // CORES
    samples = chips * CORES * OWN
    slots = chips * OWN
    positions = prompt_keys.shape[0]
    blocks = key_scale.shape[0]
    limit = suffix_key_rows.shape[1]
    depth, columns = out_weight.shape
    out_rows = samples // groups
    any_spec = pl.BlockSpec(memory_space=pl.ANY)
    return pl.pallas_call(
        functools.partial(kernel, chips, groups),
        out_shape=pltpu.VMEM((out_rows, columns), F32),
        in_specs=[any_spec] * 10,
        out_specs=pl.BlockSpec(memory_space=pltpu.VMEM),
        scratch_shapes=[
            pltpu.VMEM(queries.shape, BF16),
            pltpu.VMEM((1, samples), jnp.int32),
            pltpu.SMEM((OWN,), jnp.int32),
            pltpu.VMEM((CORES, positions, WIDTH), BF16),
            pltpu.VMEM((CORES, positions, WIDTH), BF16),
            pltpu.VMEM((1, blocks), F32),
            pltpu.VMEM((1, blocks), F32),
            pltpu.VMEM((CORES, 2 * blocks, WIDTH), F32),
            pltpu.VMEM((OWN, limit, WIDTH), BF16),
            pltpu.VMEM((OWN, limit, WIDTH), BF16),
            pltpu.VMEM((CORES, columns, depth), BF16),
            pltpu.VMEM((ROWS, WIDTH), F32),
            pltpu.VMEM((CORES, chips, ROWS, WIDTH), BF16),
            pltpu.VMEM((samples * GROUP, WIDTH), F32),
            pltpu.VMEM((slots * GROUP, WIDTH), F32),
            pltpu.VMEM((slots * GROUP, WIDTH), BF16),
            pltpu.VMEM((chips, 1, WIDTH), F32),
            pltpu.VMEM((chips, ROWS, WIDTH), BF16),
            pltpu.VMEM((chips, 1, WIDTH), F32),
            pltpu.VMEM((chips, ROWS, WIDTH), BF16),
            pltpu.VMEM((groups, slots // groups * GROUP, WIDTH), F32),
            pltpu.VMEM((CORES, groups, slots // groups, columns), F32),
            pltpu.VMEM((CORES * groups, slots // groups, columns), F32),
            pltpu.SemaphoreType.DMA((10,)),
            pltpu.SemaphoreType.DMA((10,)),
            pltpu.SemaphoreType.DMA((10,)),
            pltpu.SemaphoreType.DMA((chips // ROW_CHIPS,)),
        ],
        compiler_params=pltpu.CompilerParams(
            collective_id=0, has_side_effects=True, vmem_limit_bytes=60 * 1024 * 1024
        ),
        name="decode_attention",
    )(
        queries,
        owner_slot.reshape(1, samples),
        suffix_len,
        prompt_keys,
        prompt_value_rows,
        key_scale.reshape(1, blocks),
        value_block_scale.reshape(1, blocks),
        suffix_key_rows,
        suffix_value_rows,
        out_weight.T,
    )


def solution(mesh):
    in_specs = (
        P("seq", "kv"),
        P(),
        P("seq"),
        P("seq", "kv"),
        P("seq", "kv"),
        P("seq", "kv"),
        P("seq", "kv"),
        P("seq", None, "kv"),
        P("seq", None, "kv"),
        P("kv", "seq"),
    )
    out_specs = P("kv", "seq")
    return jax.shard_map(local, mesh=mesh, in_specs=in_specs, out_specs=out_specs, check_vma=False)
```

```python
import functools

import jax
import jax.numpy as jnp
from jax import lax
from jax.experimental import pallas as pl
from jax.experimental.pallas import tpu as pltpu
from jax.sharding import PartitionSpec as P

MESH = pl.DeviceIdType.MESH
F32 = jnp.float32
BF16 = jnp.bfloat16
LOG2E = 1.4426950408889634
NEG_FILL = -1e30

CORES = 2
ROW_CHIPS = 4
GROUP = 8
WIDTH = 128
OWN = 2
ROWS = OWN * GROUP
SPAN = 128

SQ, SC, SK, SV, SW, SF, SN, SS, SA, SY = range(10)
LQ, LO, LK, LV, LKS, LVS, LW, LSK, LSV, LSL = range(10)


def nt_dot(a, b):
    return lax.dot_general(a, b, (((1,), (1,)), ((), ())), preferred_element_type=F32)


def near_pairs(size):
    pairs = [[0]] + [[step, size - step] for step in range(1, size // 2)] + [[size // 2]]
    places = iter(range(size))
    return [[(next(places), k) for k in pair] for pair in pairs]


def kernel(
    chips,
    groups,
    q_hbm,
    os_hbm,
    sl_hbm,
    k_hbm,
    v_hbm,
    ks_hbm,
    vs_hbm,
    sk_hbm,
    sv_hbm,
    w_hbm,
    o_ref,
    qown,
    osv,
    sls,
    kbuf,
    vbuf,
    ksv,
    vsv,
    scb,
    skb,
    svb,
    wbuf,
    q32,
    qg,
    qf32,
    qs32,
    nsend,
    ssend,
    nrecv,
    srecv,
    att,
    a32,
    ysend,
    yrecv,
    ssem,
    rsem,
    lsem,
    asem,
):
    me = lax.axis_index("seq")
    y = lax.axis_index("kv")
    c = lax.rem(me, CORES)
    chip = me // CORES
    other = 1 - c
    depth_chips = chips // ROW_CHIPS

    def load(src, dst, i):
        cp = pltpu.make_async_copy(src, dst, lsem.at[i])
        cp.start()
        return cp

    def remote(src, dst, i, seq, kv):
        return pltpu.make_async_remote_copy(
            src_ref=src,
            dst_ref=dst,
            send_sem=ssem.at[i],
            recv_sem=rsem.at[i],
            device_id={"kv": kv, "seq": seq},
            device_id_type=MESH,
        )

    load_q = load(q_hbm, qown, LQ)

    def far_first(k):
        a, b = k // ROW_CHIPS, lax.rem(k, ROW_CHIPS)
        return lax.rem(chip // ROW_CHIPS + far_offset(a, depth_chips), depth_chips) * ROW_CHIPS + far_in_row(b)

    def far_in_row(b):
        return lax.rem(chip + far_offset(b, ROW_CHIPS), ROW_CHIPS)

    def far_offset(k, size):
        step = jnp.where(lax.rem(k, 2) == 0, size // 2 - k // 2, size // 2 + (k + 1) // 2)
        return jnp.where(k == size - 1, 0, step)

    barrier = pltpu.get_barrier_semaphore()

    def greet(seq, kv):
        pl.semaphore_signal(barrier, inc=1, device_id={"kv": kv, "seq": seq}, device_id_type=MESH)

    def greet_plane(k, carry):
        greet(far_first(k) * CORES + c, y)
        return carry

    lax.fori_loop(0, chips - 1, greet_plane, 0, unroll=True)

    def greet_column(k, carry):
        kv = lax.rem(y + far_offset(k, groups), groups)
        greet(chip * CORES + c, kv)
        greet(chip * CORES + other, kv)
        return carry

    lax.fori_loop(0, groups - 1, greet_column, 0, unroll=True)
    greet(chip * CORES + other, y)

    load_o = load(os_hbm, osv, LO)
    load_ks = load(ks_hbm, ksv, LKS)
    load_vs = load(vs_hbm, vsv, LVS)
    load_k = load(k_hbm, kbuf.at[c], LK)
    load_v = load(v_hbm, vbuf.at[c], LV)
    load_w = load(w_hbm, wbuf.at[c], LW)
    load_sk = load(sk_hbm, skb, LSK)
    load_sv = load(sv_hbm, svb, LSV)
    load_sl = load(sl_hbm, sls, LSL)

    load_q.wait()
    for h in range(GROUP):
        piece = qown[:, h * WIDTH : (h + 1) * WIDTH].astype(F32)
        for s in range(OWN):
            q32[s * GROUP + h : s * GROUP + h + 1, :] = piece[s : s + 1, :]
    qg[c, chip] = q32[...].astype(BF16)

    pl.semaphore_wait(barrier, (chips - 1) + 2 * (groups - 1) + 1)

    def send_queries(k, carry):
        remote(qg.at[c, chip], qg.at[c, chip], SQ, far_first(k) * CORES + c, y).start()
        return carry

    lax.fori_loop(0, chips - 1, send_queries, 0, unroll=True)

    partner = chip * CORES + other
    swap_k = remote(k_hbm, kbuf.at[c], SK, partner, y)
    swap_k.start()
    swap_v = remote(v_hbm, vbuf.at[c], SV, partner, y)
    swap_v.start()
    swap_w = remote(w_hbm, wbuf.at[c], SW, partner, y)
    swap_w.start()
    load_ks.wait()
    load_vs.wait()
    blocks = ksv.shape[1]
    scb[c, 0:blocks, :] = jnp.concatenate(
        [jnp.broadcast_to(ksv[:, b : b + 1] * (WIDTH**-0.5 * LOG2E), (1, WIDTH)) for b in range(blocks)], axis=0
    )
    scb[c, blocks : 2 * blocks, :] = jnp.concatenate(
        [jnp.broadcast_to(vsv[:, b : b + 1], (1, WIDTH)) for b in range(blocks)], axis=0
    )
    swap_f = remote(scb.at[c], scb.at[c], SF, partner, y)
    swap_f.start()

    load_o.wait()
    samples = chips * CORES * OWN
    slots = chips * OWN
    s_i = lax.broadcasted_iota(jnp.int32, (samples, samples), 0)
    m_i = lax.broadcasted_iota(jnp.int32, (samples, samples), 1)
    m_in = lax.rem(m_i, slots)
    s_of_m = (m_in // OWN) * (CORES * OWN) + (m_i // slots) * OWN + lax.rem(m_i, OWN)
    spread = jnp.where(s_i == s_of_m, 1.0, 0.0).astype(BF16)
    owner_rows = jnp.broadcast_to(osv[...].astype(F32), (16, samples)).astype(BF16)
    owner = jnp.dot(owner_rows, spread, preferred_element_type=F32)[0:1, :]
    i_i = lax.broadcasted_iota(jnp.int32, (slots, samples), 0)
    slot_i = (i_i // OWN) * (CORES * OWN) + c * OWN + lax.rem(i_i, OWN)
    pick = jnp.where(owner == slot_i.astype(F32), 1.0, 0.0).astype(BF16)

    many_q = qg.at[0, pl.ds(0, chips - 1)]
    remote(many_q, many_q, SQ, partner, y).wait_recv()
    swap_q = remote(qg.at[c], qg.at[c], SC, partner, y)
    swap_q.start()
    swap_q.wait_recv()

    qf32[...] = qg[...].reshape(samples * GROUP, WIDTH).astype(F32)
    by_head = jnp.concatenate(
        [qf32[pl.ds(h, samples, stride=GROUP), :].astype(BF16) for h in range(GROUP)], axis=1
    )
    picked = jnp.dot(pick, by_head, preferred_element_type=F32)
    for h in range(GROUP):
        qs32[pl.ds(h, slots, stride=GROUP), :] = picked[:, h * WIDTH : (h + 1) * WIDTH]

    load_k.wait()
    load_v.wait()
    swap_k.wait_recv()
    swap_v.wait_recv()
    swap_f.wait_recv()

    chunk_chips = ROW_CHIPS
    chunk = chunk_chips * ROWS
    chunks = chips // chunk_chips
    row_in = lax.rem(lax.broadcasted_iota(jnp.int32, (chunk, WIDTH), 0), ROWS)
    lane = lax.broadcasted_iota(jnp.int32, (chunk, WIDTH), 1)

    def prompt_chunk(n):
        first = pl.multiple_of(n * chunk, chunk)
        qc = qs32[pl.ds(first, chunk), :].astype(BF16)
        parts = []
        for core in range(CORES):
            s = nt_dot(qc, kbuf[core])
            for b in range(blocks):
                parts.append(s[:, b * SPAN : (b + 1) * SPAN] * scb[core, b : b + 1, :])
        peak = functools.reduce(jnp.maximum, parts)
        peak = jnp.max(peak, axis=1, keepdims=True)
        parts = [jnp.exp2(s - peak) for s in parts]
        total = jnp.sum(functools.reduce(jnp.add, parts), axis=1, keepdims=True)
        numer = None
        for core in range(CORES):
            scaled = jnp.concatenate(
                [
                    (parts[core * blocks + b] * scb[core, blocks + b : blocks + b + 1, :]).astype(BF16)
                    for b in range(blocks)
                ],
                axis=1,
            )
            term = jnp.dot(scaled, vbuf[core], preferred_element_type=F32)
            numer = term if numer is None else numer + term
        nsend[pl.ds(first, chunk), :] = numer.astype(BF16)
        stats = jnp.where(lane == row_in, peak, 0.0) + jnp.where(lane == row_in + ROWS, total, 0.0)
        stats = jnp.sum(stats.reshape(chunk_chips, ROWS, WIDTH), axis=1)
        for i in range(chunk_chips):
            ssend[n * chunk_chips + i] = stats[i : i + 1, :]

    def send_partial(t):
        first = pl.multiple_of(t * ROWS, ROWS)
        remote(ssend.at[t], srecv.at[chip], SS, t * CORES + c, y).start()
        remote(nsend.at[pl.ds(first, ROWS)], nrecv.at[chip], SN, t * CORES + c, y).start()

    own_chunk = chip // chunk_chips

    def chunk_step(k, carry):
        n = lax.rem(own_chunk + far_offset(k, chunks), chunks)
        prompt_chunk(n)

        def send_one(i, inner):
            t = n * chunk_chips + far_in_row(i)

            @pl.when(t != chip)
            def _():
                send_partial(t)

            return inner

        lax.fori_loop(0, chunk_chips, send_one, 0, unroll=True)
        return carry

    lax.fori_loop(0, chunks, chunk_step, 0)
    own_first = pl.multiple_of(chip * ROWS, ROWS)
    nrecv[chip] = nsend[pl.ds(own_first, ROWS), :]
    srecv[chip] = ssend[chip]

    load_sk.wait()
    load_sv.wait()
    load_sl.wait()
    own_q = qs32[pl.ds(own_first, ROWS), :].astype(BF16)
    limit = skb.shape[1]
    live_i = lax.broadcasted_iota(jnp.int32, (GROUP, limit), 1)
    near_numer, near_peak, near_total = [], [], []
    for j in range(OWN):
        live = live_i < sls[j]
        s = nt_dot(own_q, skb[j])[j * GROUP : (j + 1) * GROUP, :] * (WIDTH**-0.5 * LOG2E)
        s = jnp.where(live, s, NEG_FILL)
        peak = jnp.max(s, axis=1, keepdims=True)
        w = jnp.where(live, jnp.exp2(s - peak), 0.0)
        near_total.append(jnp.sum(w, axis=1, keepdims=True))
        near_peak.append(peak)
        w16 = jnp.concatenate([w, jnp.zeros_like(w)], axis=0).astype(BF16)
        near_numer.append(jnp.dot(w16, svb[j], preferred_element_type=F32)[:GROUP])
    near_numer = jnp.concatenate(near_numer, axis=0)
    near_peak = jnp.concatenate(near_peak, axis=0)
    near_total = jnp.concatenate(near_total, axis=0)

    many_s = srecv.at[pl.ds(0, chips - 1)]
    remote(many_s, many_s, SS, partner, y).wait_recv()
    stats = srecv[...].reshape(chips, WIDTH)
    stats = jnp.concatenate([stats, jnp.zeros((WIDTH - chips, WIDTH), F32)], axis=0)
    stats = jnp.transpose(stats)
    peaks = stats[0:ROWS, 0:chips]
    totals = stats[ROWS : 2 * ROWS, 0:chips]
    peak = jnp.maximum(jnp.max(peaks, axis=1, keepdims=True), near_peak)
    factor = jnp.exp2(peaks - peak)
    near_factor = jnp.exp2(near_peak - peak)
    total = jnp.sum(factor * totals, axis=1, keepdims=True) + near_total * near_factor
    many_n = nrecv.at[pl.ds(0, chips - 1)]
    remote(many_n, many_n, SN, partner, y).wait_recv()
    chains = [near_numer * near_factor] + [None] * 3
    for i in range(chips):
        term = nrecv[i].astype(F32) * factor[:, i : i + 1]
        chains[i % 4] = term if chains[i % 4] is None else chains[i % 4] + term
    numer = (chains[0] + chains[1]) + (chains[2] + chains[3])
    att[chip] = (numer * (1.0 / total)).astype(BF16)

    row = chip // ROW_CHIPS

    def send_att(to, t):
        pltpu.make_async_remote_copy(
            src_ref=att.at[chip],
            dst_ref=att.at[chip],
            send_sem=ssem.at[SA],
            recv_sem=asem.at[lax.rem(to - row + depth_chips, depth_chips)],
            device_id={"kv": y, "seq": t * CORES + c},
            device_id_type=MESH,
        ).start()

    for to in range(depth_chips):
        for b in range(ROW_CHIPS):
            t = to * ROW_CHIPS + b
            pl.when(t != chip)(functools.partial(send_att, to, t))
    load_w.wait()
    swap_w.wait_recv()
    per_group = ROW_CHIPS * OWN
    for pair in near_pairs(depth_chips):
        ts = [lax.rem(row + depth_chips - k, depth_chips) for _, k in pair]
        for (n, k), t in zip(pair, ts):
            arrived = att.at[pl.ds(0, ROW_CHIPS - (k == 0))]
            pltpu.make_async_remote_copy(
                src_ref=arrived,
                dst_ref=arrived,
                send_sem=ssem.at[SA],
                recv_sem=asem.at[k],
                device_id={"kv": y, "seq": partner},
                device_id_type=MESH,
            ).wait_recv()
            first = pl.multiple_of(t * ROW_CHIPS, ROW_CHIPS)
            a32[n] = att[pl.ds(first, ROW_CHIPS)].reshape(per_group * GROUP, WIDTH).astype(F32)
        rows = jnp.concatenate(
            [
                jnp.concatenate([a32[n, pl.ds(h, per_group, stride=GROUP), :] for n, _ in pair], axis=0).astype(BF16)
                for h in range(GROUP)
            ],
            axis=1,
        )
        for core in range(CORES):
            part = nt_dot(rows, wbuf[core])
            for m, (n, _) in enumerate(pair):
                ysend[core, n] = part[m * per_group : (m + 1) * per_group, :]
        for (n, _), t in zip(pair, ts):
            remote(ysend.at[other, n], yrecv.at[c * groups + y], SY, chip * CORES + other, t).start()

            @pl.when(t != y)
            def _():
                remote(ysend.at[c, n], yrecv.at[c * groups + y], SY, chip * CORES + c, t).start()

            @pl.when(t == y)
            def _():
                yrecv[c * groups + y] = ysend[c, n]

    many_y = yrecv.at[pl.ds(0, CORES * groups - 1)]
    last = remote(many_y, many_y, SY, partner, y)
    last.wait_recv()
    for core in range(CORES):
        acc = yrecv[core * groups]
        for i in range(1, groups):
            acc = acc + yrecv[core * groups + i]
        for q in range(per_group // OWN):
            first = q * CORES * OWN + core * OWN
            o_ref[first : first + OWN, :] = acc[q * OWN : (q + 1) * OWN, :]

    remote(many_q, many_q, SQ, partner, y).wait_send()
    swap_q.wait_send()
    swap_k.wait_send()
    swap_v.wait_send()
    swap_w.wait_send()
    swap_f.wait_send()
    remote(many_s, many_s, SS, partner, y).wait_send()
    remote(many_n, many_n, SN, partner, y).wait_send()
    many_a = att.at[pl.ds(0, chips - 1)]
    remote(many_a, many_a, SA, partner, y).wait_send()
    last.wait_send()


def local(
    queries,
    owner_slot,
    suffix_len,
    prompt_keys,
    prompt_value_rows,
    key_scale,
    value_block_scale,
    suffix_key_rows,
    suffix_value_rows,
    out_weight,
):
    groups = lax.axis_size("kv")
    chips = lax.axis_size("seq") // CORES
    samples = chips * CORES * OWN
    slots = chips * OWN
    positions = prompt_keys.shape[0]
    blocks = key_scale.shape[0]
    limit = suffix_key_rows.shape[1]
    depth, columns = out_weight.shape
    out_rows = samples // groups
    any_spec = pl.BlockSpec(memory_space=pl.ANY)
    return pl.pallas_call(
        functools.partial(kernel, chips, groups),
        out_shape=pltpu.VMEM((out_rows, columns), F32),
        in_specs=[any_spec] * 10,
        out_specs=pl.BlockSpec(memory_space=pltpu.VMEM),
        scratch_shapes=[
            pltpu.VMEM(queries.shape, BF16),
            pltpu.VMEM((1, samples), jnp.int32),
            pltpu.SMEM((OWN,), jnp.int32),
            pltpu.VMEM((CORES, positions, WIDTH), BF16),
            pltpu.VMEM((CORES, positions, WIDTH), BF16),
            pltpu.VMEM((1, blocks), F32),
            pltpu.VMEM((1, blocks), F32),
            pltpu.VMEM((CORES, 2 * blocks, WIDTH), F32),
            pltpu.VMEM((OWN, limit, WIDTH), BF16),
            pltpu.VMEM((OWN, limit, WIDTH), BF16),
            pltpu.VMEM((CORES, columns, depth), BF16),
            pltpu.VMEM((ROWS, WIDTH), F32),
            pltpu.VMEM((CORES, chips, ROWS, WIDTH), BF16),
            pltpu.VMEM((samples * GROUP, WIDTH), F32),
            pltpu.VMEM((slots * GROUP, WIDTH), F32),
            pltpu.VMEM((slots * GROUP, WIDTH), BF16),
            pltpu.VMEM((chips, 1, WIDTH), F32),
            pltpu.VMEM((chips, ROWS, WIDTH), BF16),
            pltpu.VMEM((chips, 1, WIDTH), F32),
            pltpu.VMEM((chips, ROWS, WIDTH), BF16),
            pltpu.VMEM((groups, slots // groups * GROUP, WIDTH), F32),
            pltpu.VMEM((CORES, groups, slots // groups, columns), F32),
            pltpu.VMEM((CORES * groups, slots // groups, columns), F32),
            pltpu.SemaphoreType.DMA((10,)),
            pltpu.SemaphoreType.DMA((10,)),
            pltpu.SemaphoreType.DMA((10,)),
            pltpu.SemaphoreType.DMA((chips // ROW_CHIPS,)),
        ],
        compiler_params=pltpu.CompilerParams(
            collective_id=0, has_side_effects=True, vmem_limit_bytes=60 * 1024 * 1024
        ),
        name="decode_attention",
    )(
        queries,
        owner_slot.reshape(1, samples),
        suffix_len,
        prompt_keys,
        prompt_value_rows,
        key_scale.reshape(1, blocks),
        value_block_scale.reshape(1, blocks),
        suffix_key_rows,
        suffix_value_rows,
        out_weight.T,
    )


def solution(mesh):
    in_specs = (
        P("seq", "kv"),
        P(),
        P("seq"),
        P("seq", "kv"),
        P("seq", "kv"),
        P("seq", "kv"),
        P("seq", "kv"),
        P("seq", None, "kv"),
        P("seq", None, "kv"),
        P("kv", "seq"),
    )
    out_specs = P("kv", "seq")
    return jax.shard_map(local, mesh=mesh, in_specs=in_specs, out_specs=out_specs, check_vma=False)
```
